256 devices in a mesh: section: 8 (over z_lo, y), ctx: 32 (over x, z_hi, core).
Axes of the slice: x: 4, y: 4, z: 8 (z_hi: 4, z_lo: 2; z = z_hi * 2 + z_lo), core: 2. Of those that a mesh axis runs over, the one named last changes fastest.
Arguments:
- layer_input: bfloat16 [8, 6144, 5120], P('section', 'ctx'), may hold values from -7 to 7
- self_q: bfloat16 [6144, 640], P('ctx'), may hold values from -10 to 10
- self_kv: bfloat16 [6144, 256], P('ctx'), may hold values from -10 to 10
- self_out_weight: bfloat16 [640, 5120], P(None, ('section', 'ctx')), may hold values from -0.25 to 0.25
- kv_weight: bfloat16 [5120, 256], P(('section', 'ctx')), may hold values from -0.078125 to 0.078125
- q_weight: bfloat16 [8, 5120, 640], P('section', 'ctx'), may hold values from -5 to 5
- out_weight: bfloat16 [8, 640, 5120], P('section', None, 'ctx'), may hold values from -0.25 to 0.25
Outputs:
- updates: bfloat16 [8, 6144, 5120], P('section', 'ctx')
- shared_kv: bfloat16 [6144, 256], P('ctx')
The draws below stay inside these ranges and needn't reach their ends.
All inputs are finite; a program needn't handle non-finite values.
Results may differ from the reference program's by a relative error of at most 0.0247.
Values may be sent and summed in bfloat16 or wider, within the bound.
A program may use at most 128 MiB of HBM per device.

```python
import math
import jax
import jax.numpy as jnp
from jax import lax

D = 5120
HEAD_DIM = 128
GROUP_HEADS = 5
TOK_DEV = 192
WINDOW = 128
TOKENS = 6144
LAYERS = 8
N_CTX = 32


def sign_field(key, shape):
    return jnp.where(jax.random.bernoulli(key, 0.5, shape), 1.0, -1.0).astype(jnp.float32)


def window_plan(key):
    blocks = TOKENS // TOK_DEV
    subkeys = jax.random.split(jax.random.fold_in(key, 101), 4)
    offset = jax.random.randint(subkeys[0], (blocks,), 1, TOK_DEV)
    places = jnp.arange(blocks, dtype=jnp.int32) * TOK_DEV + offset
    strength_index = jax.random.randint(subkeys[1], (blocks,), 0, 3)
    target = jnp.where(strength_index == 0, 120.0, jnp.where(strength_index == 1, 210.0, 320.0)).astype(jnp.float32)
    amount = jnp.sqrt(target / math.sqrt(HEAD_DIM))
    direction = sign_field(subkeys[2], (blocks, HEAD_DIM))
    coordinate = jax.random.randint(subkeys[3], (blocks,), 0, HEAD_DIM)
    return (places, amount, direction, coordinate)


def cross_plan(key):
    subkey = jax.random.fold_in(key, 202)
    return jax.random.permutation(subkey, D)[:3]


def draw_self_q(key, part):
    places, amount, direction, coordinate = window_plan(key)
    key = jax.random.fold_in(key, 1)
    shape = (TOKENS, GROUP_HEADS * HEAD_DIM)
    field = jax.random.truncated_normal(key, -6.0, 6.0, shape, jnp.float32)
    planted = jnp.tile(amount[:, None] * direction, (1, GROUP_HEADS))
    return field.at[places].set(planted).astype(jnp.bfloat16)


def draw_self_kv(key, part):
    places, amount, direction, coordinate = window_plan(key)
    key = jax.random.fold_in(key, 2)
    shape = (TOKENS, 2 * HEAD_DIM)
    field = jax.random.truncated_normal(key, -6.0, 6.0, shape, jnp.float32)
    near_key = amount[:, None] * direction
    shift_size = 2.0 * math.sqrt(HEAD_DIM) / amount
    marker = jnp.arange(HEAD_DIM, dtype=jnp.int32)[None, :] == coordinate[:, None]
    rival_key = near_key - jnp.where(marker, shift_size[:, None] * direction, 0.0)
    field = field.at[places, :HEAD_DIM].set(near_key)
    field = field.at[places - 1, :HEAD_DIM].set(rival_key)
    return field.astype(jnp.bfloat16)


def draw_layer_input(key, part):
    columns = cross_plan(key)
    key = jax.random.fold_in(key, 3)
    subkeys = jax.random.split(key, 5)
    shape = (LAYERS, TOKENS, D)
    field = jax.random.truncated_normal(subkeys[0], -6.0, 6.0, shape, jnp.float32)
    chosen = jnp.any(jnp.arange(D, dtype=jnp.int32)[:, None] == columns[None, :], axis=1)
    field = field * jnp.where(chosen, 0.004, 1.0).astype(jnp.float32)
    blocks = TOKENS // TOK_DEV
    offset = jax.random.randint(subkeys[1], (LAYERS, blocks), 0, TOK_DEV)
    places = jnp.arange(blocks, dtype=jnp.int32)[None, :] * TOK_DEV + offset
    column_index = jax.random.randint(subkeys[2], (LAYERS, blocks), 0, 3)
    height = jax.random.uniform(subkeys[3], (LAYERS, blocks), jnp.float32, 1.0, 6.0) * sign_field(subkeys[4], (LAYERS, blocks))
    target_column = columns[column_index]
    planted = jnp.where(jnp.arange(D, dtype=jnp.int32)[None, None, :] == target_column[:, :, None], height[:, :, None], 0.0)
    layer_rows = jnp.arange(LAYERS, dtype=jnp.int32)[:, None] * jnp.ones((1, blocks), jnp.int32)
    field = field.at[layer_rows, places].set(planted)
    return field.astype(jnp.bfloat16)


def draw_q_weight(key, part):
    columns = cross_plan(key)
    key = jax.random.fold_in(key, 4)
    subkeys = jax.random.split(key, 2)
    shape = (LAYERS, D, GROUP_HEADS * HEAD_DIM)
    field = jax.random.truncated_normal(subkeys[0], -6.0, 6.0, shape, jnp.float32) / math.sqrt(D)
    strength = jnp.array([30.0, 45.0, 65.0], jnp.float32) / math.sqrt(D)
    planted = strength[None, :, None] * sign_field(subkeys[1], (LAYERS, 3, GROUP_HEADS * HEAD_DIM))
    field = field.at[:, columns, :].set(planted)
    return field.astype(jnp.bfloat16)


def steps_of(own_key, shape, cuts, smallest, largest):
    level = 1.0
    for position, parts in cuts:
        steps = jax.random.uniform(jax.random.fold_in(jax.random.fold_in(own_key, 6), position), (parts,), jnp.float32, smallest / len(cuts), largest / len(cuts))
        level = level * jnp.repeat(jnp.exp(steps), shape[position] // parts).reshape((-1,) + (1,) * (len(shape) - 1 - position))
    return level


def bell_draw(stream_key, extent, width, bound, cuts=(), kind=jnp.bfloat16):
    values = width * jax.random.normal(stream_key, extent, jnp.float32)
    if cuts:
        values = values * steps_of(stream_key, extent, cuts, -0.22, 0.18)
    return jnp.clip(values, -bound, bound).astype(kind)


def setup_inputs(seed: int = 0) -> dict:
    arg_keys = jax.random.split(jax.random.key(seed), 8)
    return {
        "layer_input": draw_layer_input(jax.random.fold_in(arg_keys[7], 71), 0),
        "self_q": draw_self_q(jax.random.fold_in(arg_keys[7], 71), 0),
        "self_kv": draw_self_kv(jax.random.fold_in(arg_keys[7], 71), 0),
        "self_out_weight": bell_draw(arg_keys[3], (GROUP_HEADS * HEAD_DIM, D), (GROUP_HEADS * HEAD_DIM) ** -0.5, 0.25, ((1, 256),)),
        "kv_weight": bell_draw(arg_keys[4], (D, 2 * HEAD_DIM), D ** -0.5, 0.078125, ((0, 256),)),
        "q_weight": draw_q_weight(jax.random.fold_in(arg_keys[7], 71), 0),
        "out_weight": bell_draw(arg_keys[6], (LAYERS, GROUP_HEADS * HEAD_DIM, D), (GROUP_HEADS * HEAD_DIM) ** -0.5, 0.25, ((0, 8), (2, 32))),
    }


def rms_scale(values):
    return lax.rsqrt(lax.optimization_barrier(jnp.mean(values * values, axis=-1, keepdims=True)) + 1e-06)

def attend_block(queries, keys, values, query_pos, key_pos, reach, factor):
    rows = queries.shape[0]
    grouped = queries.reshape(rows, GROUP_HEADS, HEAD_DIM).astype(jnp.float32)
    scores = jnp.einsum('bhd,kd->hbk', grouped, keys.astype(jnp.float32)) * factor
    allowed = (key_pos[None, :] <= query_pos[:, None]) & (key_pos[None, :] > query_pos[:, None] - reach) & (key_pos[None, :] >= 0)
    scores = jnp.where(allowed[None], scores, -1e+30)
    top = lax.optimization_barrier(jnp.max(scores, axis=-1, keepdims=True))
    expo = jnp.where(allowed[None], jnp.exp(scores - top), 0.0)
    weights = expo.astype(jnp.bfloat16)
    numer = jnp.einsum('hbk,kd->bhd', weights.astype(jnp.float32), values.astype(jnp.float32))
    denom = lax.optimization_barrier(jnp.sum(expo, axis=-1)).T
    return (numer / denom[:, :, None]).reshape(rows, GROUP_HEADS * HEAD_DIM).astype(jnp.bfloat16)

def reference(layer_input, self_q, self_kv, self_out_weight, kv_weight, q_weight, out_weight):
    factor = 1.0 / math.sqrt(HEAD_DIM)
    padded = jnp.concatenate([jnp.zeros((TOK_DEV, 2 * HEAD_DIM), jnp.bfloat16), self_kv], axis=0)

    def window_block(index):
        start = index * TOK_DEV
        queries = lax.dynamic_slice_in_dim(self_q, start, TOK_DEV, 0)
        near = lax.dynamic_slice_in_dim(padded, start, 2 * TOK_DEV, 0)
        query_pos = start + jnp.arange(TOK_DEV, dtype=jnp.int32)
        key_pos = start - TOK_DEV + jnp.arange(2 * TOK_DEV, dtype=jnp.int32)
        return attend_block(queries, near[:, :HEAD_DIM], near[:, HEAD_DIM:], query_pos, key_pos, WINDOW, factor)
    window_out = lax.map(window_block, jnp.arange(N_CTX, dtype=jnp.int32)).reshape(TOKENS, GROUP_HEADS * HEAD_DIM)
    mixed = jnp.dot(window_out, self_out_weight, preferred_element_type=jnp.float32).astype(jnp.bfloat16)
    raw = jnp.dot(mixed, kv_weight, preferred_element_type=jnp.float32)
    shared = (raw * rms_scale(mixed.astype(jnp.float32))).astype(jnp.bfloat16)
    keys_all = shared[:, :HEAD_DIM]
    values_all = shared[:, HEAD_DIM:]
    key_pos_all = jnp.arange(TOKENS, dtype=jnp.int32)

    def one_layer(items):
        hidden, w_query, w_out = items
        wide = hidden.astype(jnp.float32)
        normed = (wide * rms_scale(wide)).astype(jnp.bfloat16)
        queries = (jnp.dot(normed, w_query, preferred_element_type=jnp.float32) * factor).astype(jnp.bfloat16)

        def cross_block(index):
            start = index * TOK_DEV
            block = lax.dynamic_slice_in_dim(queries, start, TOK_DEV, 0)
            query_pos = start + jnp.arange(TOK_DEV, dtype=jnp.int32)
            return attend_block(block, keys_all, values_all, query_pos, key_pos_all, TOKENS + 1, 1.0)
        cross = lax.map(cross_block, jnp.arange(N_CTX, dtype=jnp.int32)).reshape(TOKENS, GROUP_HEADS * HEAD_DIM)
        return jnp.dot(cross, w_out, preferred_element_type=jnp.float32).astype(jnp.bfloat16)
    updates = lax.map(one_layer, (layer_input, q_weight, out_weight))
    return (updates, shared)
```

```python
import functools
import math

import jax
import jax.numpy as jnp
from jax import lax
from jax.experimental import pallas as pl
from jax.experimental.pallas import tpu as pltpu
from jax.sharding import PartitionSpec as P

MESH = pl.DeviceIdType.MESH
WINDOW = 128
F32 = jnp.float32
BF16 = jnp.bfloat16
NEG = -1e30

NT = (((1,), (1,)), ((), ()))
NN = (((1,), (0,)), ((), ()))

SELF_ROWS = 32
PART = 48


def dot(a, b, dims=NN):
    return lax.dot_general(a, b, dims, preferred_element_type=F32)


class Place:
    def __init__(self):
        section = lax.axis_index("section")
        ctx = lax.axis_index("ctx")
        self.at = dict(zl=section // 4, y=section % 4, x=ctx // 8, zh=(ctx // 2) % 4, co=ctx % 2)
        self.ctx = ctx
        self.section = section

    SIZE = dict(zl=2, y=4, x=4, zh=4, co=2)

    def shifted(self, axis, step):
        size = self.SIZE[axis]
        return lax.rem(self.at[axis] + (step + size), size)

    def device(self, **steps):
        c = dict(self.at)
        for axis, step in steps.items():
            c[axis] = self.shifted(axis, step)
        return (c["zl"] * 4 + c["y"], (c["x"] * 4 + c["zh"]) * 2 + c["co"])

    def ctx_device(self, step):
        return (self.section, lax.rem(self.ctx + step + 32, 32))


class Copies:
    def __init__(self, send, recv):
        self.send, self.recv = send, recv
        self.count = 0
        self.open = []

    def remote(self, src, dst, device):
        i = self.count
        self.count += 1
        copy = pltpu.make_async_remote_copy(
            src_ref=src, dst_ref=dst, send_sem=self.send.at[i], recv_sem=self.recv.at[i],
            device_id=device, device_id_type=MESH)
        copy.start()
        self.open.append(copy)
        return copy

    def local(self, src, dst):
        i = self.count
        self.count += 1
        copy = pltpu.make_async_copy(src, dst, self.send.at[i])
        copy.start()
        return copy

    def drain(self):
        for copy in self.open:
            copy.wait_send()


class Gather:
    def __init__(self, place, copies, buf, low, cut, high, first, second):
        self.place, self.copies, self.buf = place, copies, buf
        self.low, self.cut, self.high = low, cut, high
        self.first, self.second = first, second
        self.got = {}
        self.swaps = {}

    def block(self, i, j, low, high):
        x, zh = (i, j) if self.first == "x" else (j, i)
        index = self.place.shifted("x", x) * 4 + self.place.shifted("zh", zh)
        return self.buf.at[index, self.place.at["co"], pl.ds(low, high - low)]

    def put(self, key, i, j, low, high, axis, step):
        ref = self.block(i, j, low, high)
        self.got[key] = self.copies.remote(ref, ref, self.place.device(**{axis: step}))

    def start1(self):
        self.put("p", 0, 0, self.low, self.high, self.first, 1)
        self.put("n", 0, 0, self.low, self.high, self.first, -1)

    def forward1(self):
        self.got["p"].wait_recv()
        self.put("fp", -1, 0, self.low, self.cut, self.first, 1)
        self.got["n"].wait_recv()
        self.put("fn", 1, 0, self.cut, self.high, self.first, -1)

    def start2(self, i):
        if i == 2:
            self.got["fp"].wait_recv()
            self.got["fn"].wait_recv()
        self.put(("p", i), i, 0, self.low, self.high, self.second, 1)
        self.put(("n", i), i, 0, self.low, self.high, self.second, -1)

    def forward2(self, i):
        self.got["p", i].wait_recv()
        self.put(("fp", i), i, -1, self.low, self.cut, self.second, 1)
        self.got["n", i].wait_recv()
        self.put(("fn", i), i, 1, self.cut, self.high, self.second, -1)

    def finish2(self, i):
        self.got["fp", i].wait_recv()
        self.got["fn", i].wait_recv()

    def swap(self, x):
        ref = self.buf.at[pl.ds(self.place.shifted("x", x) * 4, 4), self.place.at["co"],
                          pl.ds(self.low, self.high - self.low)]
        self.swaps[x] = self.copies.remote(ref, ref, self.place.device(co=1))

    def swapped(self, x):
        self.swaps[x].wait_recv()


def eye_rows(rows, columns):
    return lax.broadcasted_iota(jnp.int32, (rows, columns), 0) == lax.broadcasted_iota(jnp.int32, (rows, columns), 1)


def kernel(x_in, q_in, kv_in, so_in, kw_in, wq_in, wo_in, out, shared,
           xv, normed, wq, wo, sw, near, kv, stage, gathered, window, qacc, queries, top, total, accum, cross, res,
           send, recv):
    place = Place()
    copies = Copies(send, recv)
    ctx = place.ctx
    at = place.at
    me = at["x"] * 4 + at["zh"]
    core = at["co"]
    rows = q_in.shape[0]
    heads = q_in.shape[1] // 128
    factor = 1.0 / math.sqrt(128)

    friends = [place.device(x=1), place.device(x=-1), place.device(x=2), place.device(zh=1), place.device(zh=-1),
               place.device(zh=2), place.device(co=1), place.ctx_device(1), place.ctx_device(-1)]
    for zl in (0, 1):
        for y in range(4):
            if zl or y:
                friends.append(place.device(zl=zl, y=y))
    barrier = pltpu.get_barrier_semaphore()
    for friend in friends:
        pl.semaphore_signal(barrier, inc=1, device_id=friend, device_id_type=MESH)

    x_copy = copies.local(x_in.at[0], xv)
    wq_copy = copies.local(wq_in.at[0], wq.at[me, core])

    pick = eye_rows(SELF_ROWS, so_in.shape[1]).astype(BF16)
    sw[me, core, :, 0:640] = dot(pick, so_in[...], NT).astype(BF16)
    sw[me, core, :, 640:896] = dot(pick, kw_in[...], NN).astype(BF16)
    near[128:320, :] = kv_in[...]
    wq_copy.wait()
    pl.semaphore_wait(barrier, len(friends))

    gs = Gather(place, copies, sw, 0, 16, 32, "zh", "x")
    qa = Gather(place, copies, wq, 0, 64, 128, "zh", "x")
    qb = Gather(place, copies, wq, 128, 144, 160, "x", "zh")
    oa = Gather(place, copies, wo, 0, 64, 128, "zh", "x")
    ob = Gather(place, copies, wo, 128, 144, 160, "x", "zh")

    rim = copies.remote(kv_in.at[pl.ds(64, 128)], near.at[pl.ds(0, 128)], place.ctx_device(1))
    gs.start1()
    gs.start2(0)
    qb.start1()
    qa.start1()
    qa.start2(0)

    wo[me, core] = dot(eye_rows(160, 160).astype(BF16), wo_in[0], NT).astype(BF16)

    gs.forward1()
    gs.start2(-1)
    gs.start2(1)
    rim.wait_recv()

    qpos = lax.broadcasted_iota(jnp.int32, (rows, 320), 0)
    kpos = lax.broadcasted_iota(jnp.int32, (rows, 320), 1) - 128
    allowed = (kpos <= qpos) & (kpos > qpos - WINDOW) & (kpos >= -rows * ctx)
    for h in range(heads):
        scores = dot(q_in[:, h * 128:(h + 1) * 128], near[:, 0:128], NT) * factor
        scores = jnp.where(allowed, scores, NEG)
        expo = jnp.where(allowed, jnp.exp(scores - jnp.max(scores, axis=1, keepdims=True)), 0.0)
        numer = dot(expo.astype(BF16), near[:, 128:256])
        window[:, h * 128:(h + 1) * 128] = (numer / jnp.sum(expo, axis=1, keepdims=True)).astype(BF16)

    gs.start2(2)
    gs.swap(0)
    qb.forward1()
    qb.start2(0)
    gs.forward2(0)
    gs.forward2(-1)
    gs.forward2(1)
    qa.forward1()
    qa.start2(-1)
    qa.start2(1)
    gs.forward2(2)
    for i in (0, -1, 1, 2):
        gs.finish2(i)
    for x in (-1, 1, 2):
        gs.swap(x)
    qb.start2(-1)
    qb.start2(1)
    for x in (0, -1, 1, 2):
        gs.swapped(x)

    weights = sw[...].reshape(32 * SELF_ROWS, 896)
    mixed = dot(window[...], weights[:, 0:640], NT).astype(BF16)
    wide = mixed.astype(F32)
    squares = jnp.sum(wide * wide, axis=1, keepdims=True)
    raw = dot(mixed, weights[:, 640:896])
    diagonal = eye_rows(PART, 128)
    for s in range(8):
        y, half = s % 4, s // 4
        stage[s, 0:PART] = raw[y * PART:(y + 1) * PART, half * 128:(half + 1) * 128]
        line = jnp.sum(jnp.where(diagonal, squares[y * PART:(y + 1) * PART], 0.0), axis=0, keepdims=True)
        stage[s, PART:PART + 8] = jnp.broadcast_to(line, (8, 128))
    mine = place.section
    reduces = []
    for zl in (0, 1):
        for y in range(4):
            if zl or y:
                to = place.device(zl=zl, y=y)
                reduces.append((copies.remote(stage.at[to[0]], gathered.at[zl * 4 + y - 1], to)))

    qb.start2(2)
    qa.forward2(0)
    qa.start2(2)

    x_copy.wait()

    def norm_rows(i, carry):
        block = pl.ds(pl.multiple_of(i * 16, 16), 16)
        hidden = xv[block, :].astype(F32)
        scale = lax.rsqrt(jnp.sum(hidden * hidden, axis=1, keepdims=True) / hidden.shape[1] + 1e-6)
        hidden = (hidden * scale).astype(BF16)
        for g in range(4):
            normed[g, block, :] = hidden[:, g * 1280:(g + 1) * 1280]
        return carry

    lax.fori_loop(0, rows // 16, norm_rows, 0)

    for r in reduces:
        r.wait_recv()
    summed = stage[mine]
    for slot in range(7):
        summed = summed + gathered[slot]
    column = jnp.sum(jnp.where(diagonal, summed[PART:PART + 1], 0.0), axis=1, keepdims=True)
    piece = (summed[0:PART] * lax.rsqrt(column / 5120.0 + 1e-6)).astype(BF16)
    half, y = at["zl"], at["y"]
    kv[half, y, core, me] = piece

    own = kv.at[half, y, core, me]
    first = [copies.remote(own, own, place.device(zh=k)) for k in (1, -1, 2)]
    qa.forward2(-1)
    qb.forward2(0)
    for c in first:
        c.wait_recv()
    own = kv.at[half, y, core, pl.ds(at["x"] * 4, 4)]
    second = [copies.remote(own, own, place.device(x=k)) for k in (1, -1, 2)]
    qa.forward2(1)
    qa.swap(0)
    oa.start1()
    ob.start1()
    qb.forward2(-1)
    qb.forward2(1)
    for c in second:
        c.wait_recv()
    own = kv.at[half, y, core]
    across = copies.remote(own, own, place.device(zl=1))
    ring = {k: copies.remote(own, own, place.device(y=k)) for k in (1, -1, 2)}
    sibling = [copies.remote(own, own, place.device(co=1))]
    qa.forward2(2)
    qb.forward2(2)
    oa.start2(0)
    other = lax.rem(half + 1, 2)
    across.wait_recv()
    theirs = kv.at[other, y, core]
    ring2 = {k: copies.remote(theirs, theirs, place.device(y=k)) for k in (1, -1, 2)}
    sibling.append(copies.remote(theirs, theirs, place.device(co=1)))
    oa.forward1()
    oa.start2(-1)
    oa.start2(1)
    ob.forward1()
    ob.start2(0)
    for i in (0, -1, 1, 2):
        qa.finish2(i)
        qb.finish2(i)
    for x in (-1, 1, 2):
        qa.swap(x)
    for x in (0, -1, 1, 2):
        qb.swap(x)

    for n, x in enumerate((0, -1, 1, 2)):
        qa.swapped(x)
        qb.swapped(x)
        where = place.shifted("x", x)
        product = dot(normed[where], wq[pl.ds(where * 4, 4)].reshape(1280, 640))
        if n == 0:
            qacc[...] = product
        else:
            qacc[...] += product
    scaled = (qacc[...] * factor).astype(BF16)
    for h in range(heads):
        queries[h] = scaled[:, h * 128:(h + 1) * 128]

    top[...] = jnp.full_like(top, NEG)
    total[...] = jnp.zeros_like(total)
    accum[...] = jnp.zeros_like(accum)
    ob.start2(-1)
    ob.start2(1)
    oa.forward2(0)
    oa.start2(2)
    ob.start2(2)

    def attend(part):
        def step(n, carry):
            c, chips = n // 2, (n % 2) * 8
            first_ctx = chips * 2 + c
            last_ctx = first_ctx + 14

            def update(masked):
                block = pl.ds(pl.multiple_of(chips, 8), 8)
                keys = kv[0, part, c, block].reshape(8 * PART, 128)
                values = kv[1, part, c, block].reshape(8 * PART, 128)
                if masked:
                    lane = lax.broadcasted_iota(jnp.int32, (1, 8 * PART), 1)
                    chip = jnp.zeros_like(lane)
                    for k in range(1, 8):
                        chip = chip + (lane >= k * PART).astype(jnp.int32)
                    position = (first_ctx + 2 * chip) * 192 + part * PART + lane - chip * PART
                    row = lax.broadcasted_iota(jnp.int32, (rows, 1), 0) + ctx * rows
                    ok = position <= row
                for h in range(heads):
                    scores = dot(queries[h], keys, NT)
                    if masked:
                        scores = jnp.where(ok, scores, NEG)
                    old = top[h]
                    new = jnp.maximum(old, jnp.max(scores, axis=1, keepdims=True))
                    expo = jnp.exp(scores - new)
                    if masked:
                        expo = jnp.where(ok, expo, 0.0)
                    fade = jnp.exp(old - new)
                    total[h] = total[h] * fade + jnp.sum(expo, axis=1, keepdims=True)
                    accum[h] = accum[h] * fade + dot(expo.astype(BF16), values)
                    top[h] = new

            @pl.when(last_ctx < ctx)
            def _():
                update(False)

            @pl.when((first_ctx <= ctx) & (last_ctx >= ctx))
            def _():
                update(True)

            return carry

        lax.fori_loop(0, 4, step, 0)

    for c in sibling:
        c.wait_recv()
    attend(y)
    oa.forward2(-1)
    ob.forward2(0)
    for n, k in enumerate((1, -1, 2)):
        part = place.shifted("y", -k)
        ring[k].wait_recv()
        ring2[k].wait_recv()
        ref = kv.at[half, part, core]
        a = copies.remote(ref, ref, place.device(co=1))
        ref = kv.at[other, part, core]
        b = copies.remote(ref, ref, place.device(co=1))
        if n == 0:
            oa.forward2(1)
            ob.forward2(-1)
        elif n == 1:
            oa.forward2(2)
            ob.forward2(1)
        else:
            ob.forward2(2)
        a.wait_recv()
        b.wait_recv()
        attend(part)
    oa.swap(0)

    for k in range(4):
        shared[k * PART:(k + 1) * PART, 0:128] = kv[0, k, core, me]
        shared[k * PART:(k + 1) * PART, 128:256] = kv[1, k, core, me]
    for h in range(heads):
        cross[:, h * 128:(h + 1) * 128] = (accum[h] / total[h]).astype(BF16)

    for i in (0, -1, 1, 2):
        oa.finish2(i)
        ob.finish2(i)
    for x in (-1, 1, 2):
        oa.swap(x)
    for x in (0, -1, 1, 2):
        ob.swap(x)

    writes = []
    for n, x in enumerate((0, -1, 1, 2)):
        oa.swapped(x)
        ob.swapped(x)
        where = place.shifted("x", x)
        for pair in range(2):
            w = wo[pl.ds(where * 4 + 2 * pair, 2)].reshape(640, 640)
            res[n * 2 + pair] = dot(cross[...], w, NT).astype(BF16)
            columns = pl.ds(pl.multiple_of((where * 2 + pair) * 640, 640), 640)
            writes.append(copies.local(res.at[n * 2 + pair], out.at[0, :, columns]))
    for w in writes:
        w.wait()
    copies.drain()


COPIES = 288


def per_device(layer_input, self_q, self_kv, self_out_weight, kv_weight, q_weight, out_weight):
    vmem = pl.BlockSpec(memory_space=pltpu.VMEM)
    hbm = pl.BlockSpec(memory_space=pl.ANY)
    tokens = self_q.shape[0]
    return pl.pallas_call(
        kernel,
        name="layer_group",
        out_shape=(jax.ShapeDtypeStruct((1, tokens, 5120), BF16), jax.ShapeDtypeStruct((tokens, 256), BF16)),
        in_specs=[hbm, vmem, vmem, vmem, vmem, hbm, vmem],
        out_specs=(hbm, vmem),
        scratch_shapes=[
            pltpu.VMEM((tokens, 5120), BF16),
            pltpu.VMEM((4, tokens, 1280), BF16),
            pltpu.VMEM((16, 2, 160, 640), BF16),
            pltpu.VMEM((16, 2, 160, 640), BF16),
            pltpu.VMEM((16, 2, SELF_ROWS, 896), BF16),
            pltpu.VMEM((320, 256), BF16),
            pltpu.VMEM((2, 4, 2, 16, PART, 128), BF16),
            pltpu.VMEM((8, PART + 8, 128), F32),
            pltpu.VMEM((7, PART + 8, 128), F32),
            pltpu.VMEM((tokens, 640), BF16),
            pltpu.VMEM((tokens, 640), F32),
            pltpu.VMEM((5, tokens, 128), BF16),
            pltpu.VMEM((5, tokens, 1), F32),
            pltpu.VMEM((5, tokens, 1), F32),
            pltpu.VMEM((5, tokens, 128), F32),
            pltpu.VMEM((tokens, 640), BF16),
            pltpu.VMEM((8, tokens, 640), BF16),
            pltpu.SemaphoreType.DMA((COPIES,)),
            pltpu.SemaphoreType.DMA((COPIES,)),
        ],
        compiler_params=pltpu.CompilerParams(
            collective_id=0, has_side_effects=True, vmem_limit_bytes=56 << 20),
    )(layer_input, self_q, self_kv, self_out_weight, kv_weight, q_weight, out_weight)


def solution(mesh):
    return jax.shard_map(
        per_device,
        mesh=mesh,
        in_specs=(
            P("section", "ctx", None),
            P("ctx", None),
            P("ctx", None),
            P(None, ("section", "ctx")),
            P(("section", "ctx"), None),
            P("section", "ctx", None),
            P("section", None, "ctx"),
        ),
        out_specs=(P("section", "ctx", None), P("ctx", None)),
        check_vma=False,
    )
```

```python
import functools
import math

import jax
import jax.numpy as jnp
from jax import lax
from jax.experimental import pallas as pl
from jax.experimental.pallas import tpu as pltpu
from jax.sharding import PartitionSpec as P

MESH = pl.DeviceIdType.MESH
WINDOW = 128
F32 = jnp.float32
BF16 = jnp.bfloat16
NEG = -1e30

NT = (((1,), (1,)), ((), ()))
NN = (((1,), (0,)), ((), ()))

SELF_ROWS = 32
PART = 48
LOW = -1e20


def dot(a, b, dims=NN):
    return lax.dot_general(a, b, dims, preferred_element_type=F32)


class Place:
    def __init__(self):
        section = lax.axis_index("section")
        ctx = lax.axis_index("ctx")
        self.at = dict(zl=section // 4, y=section % 4, x=ctx // 8, zh=(ctx // 2) % 4, co=ctx % 2)
        self.ctx = ctx
        self.section = section

    SIZE = dict(zl=2, y=4, x=4, zh=4, co=2)

    def shifted(self, axis, step):
        size = self.SIZE[axis]
        return lax.rem(self.at[axis] + (step + size), size)

    def device(self, **steps):
        c = dict(self.at)
        for axis, step in steps.items():
            c[axis] = self.shifted(axis, step)
        return (c["zl"] * 4 + c["y"], (c["x"] * 4 + c["zh"]) * 2 + c["co"])

    def ctx_device(self, step):
        return (self.section, lax.rem(self.ctx + step + 32, 32))


class Copies:
    def __init__(self, send, recv):
        self.send, self.recv = send, recv
        self.sends, self.recvs = {}, {}

    def index(self, table, name):
        return table.setdefault(name, len(table))

    def remote(self, ref, device, send, recv, dst=None):
        pltpu.make_async_remote_copy(
            src_ref=ref, dst_ref=ref if dst is None else dst,
            send_sem=self.send.at[self.index(self.sends, send)],
            recv_sem=self.recv.at[self.index(self.recvs, recv)],
            device_id=device, device_id_type=MESH).start()

    def local(self, src, dst, send):
        pltpu.make_async_copy(src, dst, self.send.at[self.index(self.sends, send)]).start()

    def arrived(self, recv, like):
        pltpu.make_async_copy(like, like, self.recv.at[self.recvs[recv]]).wait()

    def left(self, send, like):
        pltpu.make_async_copy(like, like, self.send.at[self.sends[send]]).wait()


class Gather:
    def __init__(self, name, place, copies, buf, low, cut, high, first, second):
        self.name, self.place, self.copies, self.buf = name, place, copies, buf
        self.low, self.cut, self.high = low, cut, high
        self.first, self.second = first, second

    def put(self, key, i, j, low, high, axis, step):
        x, zh = (i, j) if self.first == "x" else (j, i)
        index = self.place.shifted("x", x) * 4 + self.place.shifted("zh", zh)
        ref = self.buf.at[index, self.place.at["co"], pl.ds(low, high - low)]
        self.copies.remote(ref, self.place.device(**{axis: step}), self.name, (self.name, key))

    def like(self, blocks):
        return self.buf.at[pl.ds(0, blocks), 0, pl.ds(self.low, self.high - self.low)]

    def got(self, key, blocks):
        self.copies.arrived((self.name, key), self.like(blocks))

    def start1(self):
        self.put("near", 0, 0, self.low, self.high, self.first, 1)
        self.put("near", 0, 0, self.low, self.high, self.first, -1)

    def forward1(self):
        self.got("near", 2)
        self.put("far", -1, 0, self.low, self.cut, self.first, 1)
        self.put("far", 1, 0, self.cut, self.high, self.first, -1)

    def finish1(self):
        self.got("far", 1)

    def start2(self, i):
        self.put(("near", i), i, 0, self.low, self.high, self.second, 1)
        self.put(("near", i), i, 0, self.low, self.high, self.second, -1)

    def forward2(self, i):
        self.got(("near", i), 2)
        self.put(("far", i), i, -1, self.low, self.cut, self.second, 1)
        self.put(("far", i), i, 1, self.cut, self.high, self.second, -1)

    def finish2(self, i):
        self.got(("far", i), 1)

    def sent(self):
        self.copies.left(self.name, self.like(15))


def eye_rows(rows, columns):
    return lax.broadcasted_iota(jnp.int32, (rows, columns), 0) == lax.broadcasted_iota(jnp.int32, (rows, columns), 1)


def spread(column, width):
    return jnp.broadcast_to(column, (column.shape[0], width))


def kernel(x_in, q_in, kv_in, so_in, kw_in, wq_in, wo_in, out, shared,
           xv, normed, wq, wo, sz, sw, near, kv, stage, gathered, window, qacc, queries, top, accum, cross, res,
           send, recv):
    place = Place()
    copies = Copies(send, recv)
    ctx = place.ctx
    at = place.at
    me = at["x"] * 4 + at["zh"]
    core = at["co"]
    rows = q_in.shape[0]
    heads = q_in.shape[1] // 128
    factor = 1.0 / math.sqrt(128)
    sibling = place.device(co=1)
    columns = so_in.shape[0]

    friends = [place.device(x=1), place.device(x=-1), place.device(x=2), place.device(zh=1), place.device(zh=-1),
               place.device(zh=2), sibling, place.ctx_device(1), place.ctx_device(-1)]
    for zl in (0, 1):
        for y in range(4):
            if zl or y:
                friends.append(place.device(zl=zl, y=y))
    barrier = pltpu.get_barrier_semaphore()
    for friend in friends:
        pl.semaphore_signal(barrier, inc=1, device_id=friend, device_id_type=MESH)

    copies.local(wq_in.at[0], wq.at[me, core], "wq in")
    copies.local(x_in.at[0], xv, "x in")
    copies.local(wo_in, wo.at[me, core], "wo in")

    sz[at["zh"]] = jnp.zeros((SELF_ROWS, 896), BF16)
    sz[at["zh"], 0:columns, 0:640] = so_in[...]
    sz[at["zh"], 0:columns, 640:896] = kw_in[...]
    near[128:320, :] = kv_in[...]
    copies.left("wq in", wq.at[me, core])
    pl.semaphore_wait(barrier, len(friends))

    qa = Gather("qa", place, copies, wq, 0, 64, 128, "zh", "x")
    qb = Gather("qb", place, copies, wq, 128, 144, 160, "x", "zh")
    oa = Gather("oa", place, copies, wo, 0, 64, 128, "zh", "x")
    ob = Gather("ob", place, copies, wo, 128, 144, 160, "x", "zh")

    def swap(name, buf, x):
        copies.remote(buf.at[pl.ds(place.shifted("x", x) * 4, 4), core], sibling, name + " swap", (name, "swap", x))

    def swapped(name, buf, x):
        copies.arrived((name, "swap", x), buf.at[pl.ds(0, 4), 0])

    for k in (1, -1, 2):
        copies.remote(sz.at[at["zh"]], place.device(zh=k), "self z", "self z")
    copies.remote(kv_in.at[pl.ds(64, 128)], place.ctx_device(1), "rim", "rim", near.at[pl.ds(0, 128)])
    qb.start1()
    qa.start2(0)
    qa.start1()
    copies.arrived("rim", near.at[pl.ds(0, 128)])

    qpos = lax.broadcasted_iota(jnp.int32, (rows, 320), 0)
    kpos = lax.broadcasted_iota(jnp.int32, (rows, 320), 1) - 128
    allowed = (kpos <= qpos) & (kpos > qpos - WINDOW) & (kpos >= -rows * ctx)
    for h in range(heads):
        scores = dot(q_in[:, h * 128:(h + 1) * 128], near[:, 0:128], NT) * factor
        scores = jnp.where(allowed, scores, NEG)
        expo = jnp.exp(scores - jnp.max(scores, axis=1, keepdims=True))
        numer = dot(expo.astype(BF16), near[:, 128:256])
        window[:, h * 128:(h + 1) * 128] = (numer / jnp.sum(expo, axis=1, keepdims=True)).astype(BF16)

    copies.arrived("self z", sz.at[pl.ds(0, 3)])
    for k in range(4):
        sw[at["x"], core, k * columns:(k + 1) * columns, :] = sz[k, 0:columns, :]
    own = sw.at[at["x"], core]
    for k in (1, -1, 2):
        copies.remote(own, place.device(x=k), "self x", "self x")
    copies.remote(own, sibling, "self swap", "self swap")
    qb.forward1()
    qa.forward2(0)
    qb.start2(0)

    copies.left("x in", xv)

    def norm_rows(i, carry):
        block = pl.ds(pl.multiple_of(i * 16, 16), 16)
        hidden = xv[block, :].astype(F32)
        scale = lax.rsqrt(jnp.sum(hidden * hidden, axis=1, keepdims=True) / hidden.shape[1] + 1e-6)
        hidden = (hidden * scale).astype(BF16)
        for g in range(4):
            normed[g, block, :] = hidden[:, g * 1280:(g + 1) * 1280]
        return carry

    lax.fori_loop(0, rows // 16, norm_rows, 0)

    qa.forward1()
    qa.start2(-1)
    copies.arrived("self x", sw.at[pl.ds(0, 3), 0])
    for k in (1, -1, 2):
        copies.remote(sw.at[place.shifted("x", k), core], sibling, "self swap", "self swap")
    qb.start2(-1)
    copies.arrived("self swap", sw.at[:, 0])

    weights = sw[...].reshape(32 * columns, 896)
    mixed = dot(window[...], weights[:, 0:640], NT).astype(BF16)
    wide = mixed.astype(F32)
    squares = jnp.sum(wide * wide, axis=1, keepdims=True)
    raw = dot(mixed, weights[:, 640:896])
    diagonal = eye_rows(PART, 128)
    for s in range(8):
        y, half = s % 4, s // 4
        stage[s, 0:PART] = raw[y * PART:(y + 1) * PART, half * 128:(half + 1) * 128]
        line = jnp.sum(jnp.where(diagonal, squares[y * PART:(y + 1) * PART], 0.0), axis=0, keepdims=True)
        stage[s, PART:PART + 8] = jnp.broadcast_to(line, (8, 128))
    for zl in (0, 1):
        for y in range(4):
            if zl or y:
                to = place.device(zl=zl, y=y)
                copies.remote(stage.at[to[0]], to, "reduce", "reduce", gathered.at[zl * 4 + y - 1])

    qa.start2(1)
    qa.finish1()
    qb.start2(1)
    qa.forward2(-1)
    copies.arrived("reduce", gathered)
    summed = stage[place.section]
    for slot in range(7):
        summed = summed + gathered[slot]
    column = jnp.sum(jnp.where(diagonal, summed[PART:PART + 1], 0.0), axis=1, keepdims=True)
    half, y = at["zl"], at["y"]
    other = lax.rem(half + 1, 2)

    def group(h, part, c):
        return (h * 4 + part) * 2 + c

    mine = group(half, y, core)
    kv[mine, me] = (summed[0:PART] * lax.rsqrt(column / 5120.0 + 1e-6)).astype(BF16)

    for k in (1, -1, 2):
        copies.remote(kv.at[mine, me], place.device(zh=k), "kv piece", "kv z")
    qb.finish1()
    qb.start2(2)
    qb.forward2(0)
    copies.arrived("kv z", kv.at[0, pl.ds(0, 3)])
    for k in (1, -1, 2):
        copies.remote(kv.at[mine, pl.ds(at["x"] * 4, 4)], place.device(x=k), "kv piece", "kv x")
    qa.start2(2)
    qb.forward2(-1)
    copies.left("wo in", wo.at[me, core])
    ob.start1()
    copies.arrived("kv x", kv.at[0, pl.ds(0, 12)])

    def round_start(h):
        for k in (1, -1):
            copies.remote(kv.at[group(h, y, core)], place.device(y=k), "kv group", ("kv near", h is half))

    def round_forward(h):
        copies.arrived(("kv near", h is half), kv.at[pl.ds(0, 2)])
        copies.remote(kv.at[group(h, place.shifted("y", -1), core), pl.ds(0, 8)], place.device(y=1),
                      "kv group", ("kv far", h is half))
        copies.remote(kv.at[group(h, place.shifted("y", 1), core), pl.ds(8, 8)], place.device(y=-1),
                      "kv group", ("kv far", h is half))

    def hand(h, part, name):
        copies.remote(kv.at[group(h, part, core)], sibling, "kv swap", name)

    copies.remote(kv.at[mine], place.device(zl=1), "kv group", "kv across")
    round_start(half)
    hand(half, y, "kv swap 0")
    qa.forward2(1)
    qb.forward2(1)
    oa.start1()
    qa.forward2(2)
    qb.forward2(2)
    copies.arrived("kv across", kv.at[0])
    round_start(other)
    hand(other, y, "kv swap 0")
    oa.start2(0)
    round_forward(half)
    ob.forward1()

    top[...] = jnp.full_like(top, LOW)
    accum[...] = jnp.zeros_like(accum)

    for n, x in enumerate((0, -1, 1, 2)):
        qa.finish2(x)
    for x in (0, -1, 1, 2):
        qb.finish2(x)
    for x in (0, -1, 1, 2):
        swap("wq", wq, x)
    ob.start2(0)

    for n, x in enumerate((0, -1, 1, 2)):
        swapped("wq", wq, x)
        where = place.shifted("x", x)
        product = dot(normed[where], wq[pl.ds(where * 4, 4)].reshape(1280, 640))
        if n == 0:
            qacc[...] = product
        else:
            qacc[...] += product
    scaled = (qacc[...] * factor).astype(BF16)
    for h in range(heads):
        queries[h] = scaled[:, h * 128:(h + 1) * 128]

    lane = lax.broadcasted_iota(jnp.int32, (1, 16 * PART), 1)
    chip = jnp.zeros_like(lane)
    for k in range(1, 16):
        chip = chip + (lane >= k * PART).astype(jnp.int32)
    position0 = chip * (2 * rows) + lane - chip * PART
    row = lax.broadcasted_iota(jnp.int32, (rows, 1), 0) + ctx * rows
    ones = jnp.ones((16 * PART, 128), BF16)

    def attend(part, c):
        keys = kv[group(0, part, c)].reshape(16 * PART, 128)
        values = kv[group(1, part, c)].reshape(16 * PART, 128)
        both = jnp.concatenate([values, ones], axis=1)
        bias = jnp.where(position0 + (c * rows + part * PART) <= row, 0.0, NEG)
        for h in range(heads):
            scores = dot(queries[h], keys, NT) + bias
            old = top[h]
            new = jnp.maximum(old, spread(jnp.max(scores, axis=1, keepdims=True), 128))
            expo = jnp.exp(scores - jnp.tile(new, (1, 6)))
            fade = jnp.exp(old - new)
            accum[h] = accum[h] * jnp.tile(fade, (1, 2)) + dot(expo.astype(BF16), both)
            top[h] = new

    oa.forward1()
    oa.start2(-1)
    copies.arrived("kv swap 0", kv.at[pl.ds(0, 2)])
    attend(y, 0)
    round_forward(other)
    for h in (half, other):
        for k in (1, -1):
            hand(h, place.shifted("y", k), "kv swap 1")
    oa.start2(1)
    oa.forward2(0)
    oa.finish1()
    ob.start2(-1)
    attend(y, 1)
    oa.start2(2)
    ob.finish1()
    ob.start2(1)
    ob.start2(2)
    copies.arrived("kv swap 1", kv.at[pl.ds(0, 4)])
    attend(place.shifted("y", -1), 0)
    ob.forward2(0)
    oa.forward2(-1)
    attend(place.shifted("y", -1), 1)
    for h in (half, other):
        copies.arrived(("kv far", h is half), kv.at[0])
        hand(h, place.shifted("y", 2), "kv swap 2")
    ob.forward2(-1)
    attend(place.shifted("y", 1), 0)
    oa.forward2(1)
    ob.forward2(1)
    attend(place.shifted("y", 1), 1)
    copies.arrived("kv swap 2", kv.at[pl.ds(0, 2)])
    ob.forward2(2)
    attend(place.shifted("y", 2), 0)
    oa.forward2(2)
    attend(place.shifted("y", 2), 1)

    for h in range(heads):
        cross[:, h * 128:(h + 1) * 128] = (accum[h, :, 0:128] / accum[h, :, 128:256]).astype(BF16)
    for k in range(4):
        shared[k * PART:(k + 1) * PART, 0:128] = kv[group(0, k, core), me]
        shared[k * PART:(k + 1) * PART, 128:256] = kv[group(1, k, core), me]

    for x in (0, -1, 1, 2):
        ob.finish2(x)
    for x in (0, -1, 1, 2):
        oa.finish2(x)
        swap("wo", wo, x)
    for n, x in enumerate((0, -1, 1, 2)):
        swapped("wo", wo, x)
        where = place.shifted("x", x)
        for pair in range(2):
            w = wo[pl.ds(where * 4 + 2 * pair, 2)].reshape(640, 640)
            res[n * 2 + pair] = dot(cross[...], w, NT).astype(BF16)
            block = pl.ds(pl.multiple_of((where * 2 + pair) * 640, 640), 640)
            copies.local(res.at[n * 2 + pair], out.at[0, :, block], "out")

    for gather in (qa, qb, oa, ob):
        gather.sent()
    copies.left("wq swap", wq.at[:, 0])
    copies.left("wo swap", wo.at[:, 0])
    copies.left("self z", sz.at[pl.ds(0, 3)])
    copies.left("self x", sw.at[pl.ds(0, 3), 0])
    copies.left("self swap", sw.at[:, 0])
    copies.left("rim", near.at[pl.ds(0, 128)])
    copies.left("reduce", gathered)
    copies.left("kv piece", kv.at[0, pl.ds(0, 15)])
    copies.left("kv group", kv.at[pl.ds(0, 7)])
    copies.left("kv swap", kv.at[pl.ds(0, 8)])
    copies.left("out", res)
    assert (len(copies.sends), len(copies.recvs)) == (SENDS, RECVS), (len(copies.sends), len(copies.recvs))


SENDS = 18
RECVS = 63


def per_device(layer_input, self_q, self_kv, self_out_weight, kv_weight, q_weight, out_weight):
    vmem = pl.BlockSpec(memory_space=pltpu.VMEM)
    hbm = pl.BlockSpec(memory_space=pl.ANY)
    tokens = self_q.shape[0]
    columns = kv_weight.shape[0]
    return pl.pallas_call(
        kernel,
        name="layer_group",
        out_shape=(jax.ShapeDtypeStruct((1, tokens, 5120), BF16), jax.ShapeDtypeStruct((tokens, 256), BF16)),
        in_specs=[hbm, vmem, vmem, vmem, vmem, hbm, hbm],
        out_specs=(hbm, vmem),
        scratch_shapes=[
            pltpu.VMEM((tokens, 5120), BF16),
            pltpu.VMEM((4, tokens, 1280), BF16),
            pltpu.VMEM((16, 2, 160, 640), BF16),
            pltpu.VMEM((16, 2, 160, 640), BF16),
            pltpu.VMEM((4, SELF_ROWS, 896), BF16),
            pltpu.VMEM((4, 2, 4 * columns, 896), BF16),
            pltpu.VMEM((320, 256), BF16),
            pltpu.VMEM((16, 16, PART, 128), BF16),
            pltpu.VMEM((8, PART + 8, 128), F32),
            pltpu.VMEM((7, PART + 8, 128), F32),
            pltpu.VMEM((tokens, 640), BF16),
            pltpu.VMEM((tokens, 640), F32),
            pltpu.VMEM((5, tokens, 128), BF16),
            pltpu.VMEM((5, tokens, 128), F32),
            pltpu.VMEM((5, tokens, 256), F32),
            pltpu.VMEM((tokens, 640), BF16),
            pltpu.VMEM((8, tokens, 640), BF16),
            pltpu.SemaphoreType.DMA((SENDS,)),
            pltpu.SemaphoreType.DMA((RECVS,)),
        ],
        compiler_params=pltpu.CompilerParams(
            collective_id=0, has_side_effects=True, vmem_limit_bytes=56 << 20),
    )(layer_input, self_q, self_kv, self_out_weight.T, kv_weight, q_weight, out_weight[0].T)


def solution(mesh):
    return jax.shard_map(
        per_device,
        mesh=mesh,
        in_specs=(
            P("section", "ctx", None),
            P("ctx", None),
            P("ctx", None),
            P(None, ("section", "ctx")),
            P(("section", "ctx"), None),
            P("section", "ctx", None),
            P("section", None, "ctx"),
        ),
        out_specs=(P("section", "ctx", None), P("ctx", None)),
        check_vma=False,
    )
```

```python
import functools
import math

import jax
import jax.numpy as jnp
from jax import lax
from jax.experimental import pallas as pl
from jax.experimental.pallas import tpu as pltpu
from jax.sharding import PartitionSpec as P

MESH = pl.DeviceIdType.MESH
WINDOW = 128
F32 = jnp.float32
BF16 = jnp.bfloat16
NEG = -1e30

NT = (((1,), (1,)), ((), ()))
NN = (((1,), (0,)), ((), ()))

SELF_ROWS = 32
PART = 48
LOW = -1e20


def dot(a, b, dims=NN):
    return lax.dot_general(a, b, dims, preferred_element_type=F32)


class Place:
    def __init__(self):
        section = lax.axis_index("section")
        ctx = lax.axis_index("ctx")
        self.at = dict(zl=section // 4, y=section % 4, x=ctx // 8, zh=(ctx // 2) % 4, co=ctx % 2)
        self.ctx = ctx
        self.section = section

    SIZE = dict(zl=2, y=4, x=4, zh=4, co=2)

    def shifted(self, axis, step):
        size = self.SIZE[axis]
        return lax.rem(self.at[axis] + (step + size), size)

    def device(self, **steps):
        c = dict(self.at)
        for axis, step in steps.items():
            c[axis] = self.shifted(axis, step)
        return (c["zl"] * 4 + c["y"], (c["x"] * 4 + c["zh"]) * 2 + c["co"])

    def ctx_device(self, step):
        return (self.section, lax.rem(self.ctx + step + 32, 32))


class Copies:
    def __init__(self, send, recv):
        self.send, self.recv = send, recv
        self.sends, self.recvs = {}, {}

    def index(self, table, name):
        return table.setdefault(name, len(table))

    def remote(self, ref, device, send, recv, dst=None):
        pltpu.make_async_remote_copy(
            src_ref=ref, dst_ref=ref if dst is None else dst,
            send_sem=self.send.at[self.index(self.sends, send)],
            recv_sem=self.recv.at[self.index(self.recvs, recv)],
            device_id=device, device_id_type=MESH).start()

    def local(self, src, dst, send):
        pltpu.make_async_copy(src, dst, self.send.at[self.index(self.sends, send)]).start()

    def arrived(self, recv, like):
        pltpu.make_async_copy(like, like, self.recv.at[self.recvs[recv]]).wait()

    def left(self, send, like):
        pltpu.make_async_copy(like, like, self.send.at[self.sends[send]]).wait()


class Gather:
    def __init__(self, name, place, copies, buf, low, cut, high, first, second):
        self.name, self.place, self.copies, self.buf = name, place, copies, buf
        self.low, self.cut, self.high = low, cut, high
        self.first, self.second = first, second

    def put(self, key, i, j, low, high, axis, step):
        x, zh = (i, j) if self.first == "x" else (j, i)
        index = self.place.shifted("x", x) * 4 + self.place.shifted("zh", zh)
        ref = self.buf.at[index, self.place.at["co"], pl.ds(low, high - low)]
        self.copies.remote(ref, self.place.device(**{axis: step}), self.name, (self.name, key))

    def like(self, blocks):
        return self.buf.at[pl.ds(0, blocks), 0, pl.ds(self.low, self.high - self.low)]

    def got(self, key, blocks):
        self.copies.arrived((self.name, key), self.like(blocks))

    def start1(self):
        self.put("near", 0, 0, self.low, self.high, self.first, 1)
        self.put("near", 0, 0, self.low, self.high, self.first, -1)

    def forward1(self):
        self.got("near", 2)
        self.put("far", -1, 0, self.low, self.cut, self.first, 1)
        self.put("far", 1, 0, self.cut, self.high, self.first, -1)

    def start2(self, i):
        if i == 2:
            self.got("far", 1)
        self.put(("near", i), i, 0, self.low, self.high, self.second, 1)
        self.put(("near", i), i, 0, self.low, self.high, self.second, -1)

    def forward2(self, i):
        self.got(("near", i), 2)
        self.put(("far", i), i, -1, self.low, self.cut, self.second, 1)
        self.put(("far", i), i, 1, self.cut, self.high, self.second, -1)

    def finish2(self, i):
        self.got(("far", i), 1)

    def sent(self):
        self.copies.left(self.name, self.like(15))


class Swap:
    def __init__(self, name, place, copies, buf):
        self.name, self.place, self.copies, self.buf = name, place, copies, buf

    def put(self, x, ref):
        self.copies.remote(ref, self.place.device(co=1), (self.name, "swap"), (self.name, "swap", x))

    def rows(self, x, low, count):
        return self.buf.at[pl.ds(self.place.shifted("x", x) * 4, 4), self.place.at["co"], pl.ds(low, count)]

    def most(self, x):
        self.put(x, self.rows(x, 0, 128))

    def far(self, i):
        index = self.place.shifted("x", 2) * 4 + self.place.shifted("zh", i)
        self.put(2, self.buf.at[index, self.place.at["co"], pl.ds(0, 128)])

    def rest(self, x):
        self.put(x, self.rows(x, 128, 32))

    def done(self, x):
        self.copies.arrived((self.name, "swap", x), self.buf.at[pl.ds(0, 4), 0])


def eye_rows(rows, columns):
    return lax.broadcasted_iota(jnp.int32, (rows, columns), 0) == lax.broadcasted_iota(jnp.int32, (rows, columns), 1)


def spread(column, width):
    return jnp.broadcast_to(column, (column.shape[0], width))


def kernel(x_in, q_hbm, kv_in, so_hbm, kw_hbm, wq_in, wo_in, out, shared,
           q_in, so_in, kw_in, xv, normed, wq, wo, sz, sw, near, kv, stage, gathered, window, qacc, queries, top, accum, cross, res,
           send, recv):
    place = Place()
    copies = Copies(send, recv)
    ctx = place.ctx
    at = place.at
    me = at["x"] * 4 + at["zh"]
    core = at["co"]
    rows = q_in.shape[0]
    heads = q_in.shape[1] // 128
    factor = 1.0 / math.sqrt(128)
    sibling = place.device(co=1)
    columns = so_in.shape[0]

    friends = [place.device(x=1), place.device(x=-1), place.device(x=2), place.device(zh=1), place.device(zh=-1),
               place.device(zh=2), sibling, place.ctx_device(1), place.ctx_device(-1)]
    for zl in (0, 1):
        for y in range(4):
            if zl or y:
                friends.append(place.device(zl=zl, y=y))
    barrier = pltpu.get_barrier_semaphore()
    for friend in friends:
        pl.semaphore_signal(barrier, inc=1, device_id=friend, device_id_type=MESH)

    copies.local(so_hbm, so_in, "so in")
    copies.local(kw_hbm, kw_in, "kw in")
    copies.local(kv_in, near.at[pl.ds(128, rows)], "kv in")
    copies.local(wq_in.at[0], wq.at[me, core], "wq in")
    copies.local(q_hbm, q_in, "q in")
    copies.local(x_in.at[0], xv, "x in")
    copies.local(wo_in, wo.at[me, core], "wo in")

    sz[at["zh"]] = jnp.zeros((SELF_ROWS, 896), BF16)
    copies.left("so in", so_in)
    copies.left("kw in", kw_in)
    sz[at["zh"], 0:columns, 0:640] = so_in[...]
    sz[at["zh"], 0:columns, 640:896] = kw_in[...]
    copies.left("kv in", near.at[pl.ds(128, rows)])
    copies.left("wq in", wq.at[me, core])
    pl.semaphore_wait(barrier, len(friends))

    qa = Gather("qa", place, copies, wq, 0, 64, 128, "zh", "x")
    qb = Gather("qb", place, copies, wq, 128, 144, 160, "x", "zh")
    oa = Gather("oa", place, copies, wo, 0, 64, 128, "zh", "x")
    ob = Gather("ob", place, copies, wo, 128, 144, 160, "x", "zh")
    half, y = at["zl"], at["y"]
    other = lax.rem(half + 1, 2)
    diagonal = eye_rows(PART, 128)

    def group(h, part, c):
        return (h * 4 + part) * 2 + c

    mine = group(half, y, core)

    q_swap = Swap("wq", place, copies, wq)
    o_swap = Swap("wo", place, copies, wo)

    def start():
        for k in (1, -1, 2):
            copies.remote(sz.at[at["zh"]], place.device(zh=k), "self z", "self z")
        copies.remote(near.at[pl.ds(192, 128)], place.ctx_device(1), "rim", "rim", near.at[pl.ds(0, 128)])

    def window_attention():
        copies.left("q in", q_in)
        copies.arrived("rim", near.at[pl.ds(0, 128)])
        qpos = lax.broadcasted_iota(jnp.int32, (rows, 320), 0)
        kpos = lax.broadcasted_iota(jnp.int32, (rows, 320), 1) - 128
        allowed = (kpos <= qpos) & (kpos > qpos - WINDOW) & (kpos >= -rows * ctx)
        for h in range(heads):
            scores = dot(q_in[:, h * 128:(h + 1) * 128], near[:, 0:128], NT) * factor
            scores = jnp.where(allowed, scores, NEG)
            expo = jnp.exp(scores - jnp.max(scores, axis=1, keepdims=True))
            numer = dot(expo.astype(BF16), near[:, 128:256])
            window[:, h * 128:(h + 1) * 128] = (numer / jnp.sum(expo, axis=1, keepdims=True)).astype(BF16)

    def self_x():
        copies.arrived("self z", sz.at[pl.ds(0, 3)])
        for k in range(4):
            sw[at["x"], core, k * columns:(k + 1) * columns, :] = sz[k, 0:columns, :]
        own = sw.at[at["x"], core]
        for k in (1, -1, 2):
            copies.remote(own, place.device(x=k), "self x", "self x")
        copies.remote(own, sibling, "self swap", "self swap")

    def self_swap():
        copies.arrived("self x", sw.at[pl.ds(0, 3), 0])
        for k in (1, -1, 2):
            copies.remote(sw.at[place.shifted("x", k), core], sibling, "self swap", "self swap")

    def mix():
        copies.arrived("self swap", sw.at[:, 0])
        weights = sw[...].reshape(32 * columns, 896)
        mixed = dot(window[...], weights[:, 0:640], NT).astype(BF16)
        wide = mixed.astype(F32)
        squares = jnp.sum(wide * wide, axis=1, keepdims=True)
        raw = dot(mixed, weights[:, 640:896])
        for s in range(8):
            part, side = s % 4, s // 4
            stage[s, 0:PART] = raw[part * PART:(part + 1) * PART, side * 128:(side + 1) * 128]
            line = jnp.sum(jnp.where(diagonal, squares[part * PART:(part + 1) * PART], 0.0), axis=0, keepdims=True)
            stage[s, PART:PART + 8] = jnp.broadcast_to(line, (8, 128))
        for zl in (0, 1):
            for k in range(4):
                if zl or k:
                    to = place.device(zl=zl, y=k)
                    copies.remote(stage.at[to[0]], to, "reduce", "reduce", gathered.at[zl * 4 + k - 1])

    def reduce():
        copies.arrived("reduce", gathered)
        summed = stage[place.section]
        for slot in range(7):
            summed = summed + gathered[slot]
        column = jnp.sum(jnp.where(diagonal, summed[PART:PART + 1], 0.0), axis=1, keepdims=True)
        kv[mine, me] = (summed[0:PART] * lax.rsqrt(column / 5120.0 + 1e-6)).astype(BF16)
        for k in (1, -1, 2):
            copies.remote(kv.at[mine, me], place.device(zh=k), "kv piece", "kv z")

    def kv_x():
        copies.arrived("kv z", kv.at[0, pl.ds(0, 3)])
        for k in (1, -1, 2):
            copies.remote(kv.at[mine, pl.ds(at["x"] * 4, 4)], place.device(x=k), "kv piece", "kv x")

    def round_start(h):
        for k in (1, -1):
            copies.remote(kv.at[group(h, y, core)], place.device(y=k), "kv group", ("kv near", h is half))

    def hand(h, part, batch):
        copies.remote(kv.at[group(h, part, core)], sibling, "kv swap", ("kv swap", batch))

    def kv_round():
        copies.arrived("kv x", kv.at[0, pl.ds(0, 12)])
        copies.remote(kv.at[mine], place.device(zl=1), "kv group", "kv across")
        round_start(half)
        hand(half, y, 0)

    def kv_across():
        copies.arrived("kv across", kv.at[0])
        round_start(other)
        hand(other, y, 0)

    def round_forward(h):
        copies.arrived(("kv near", h is half), kv.at[pl.ds(0, 2)])
        copies.remote(kv.at[group(h, place.shifted("y", -1), core), pl.ds(0, 8)], place.device(y=1),
                      "kv group", ("kv far", h is half))
        copies.remote(kv.at[group(h, place.shifted("y", 1), core), pl.ds(8, 8)], place.device(y=-1),
                      "kv group", ("kv far", h is half))
        for k in (1, -1):
            hand(h, place.shifted("y", k), 1)

    def round_end(h):
        copies.arrived(("kv far", h is half), kv.at[0])
        hand(h, place.shifted("y", 2), 2)

    def normalise():
        copies.left("x in", xv)

        def norm_rows(i, carry):
            block = pl.ds(pl.multiple_of(i * 16, 16), 16)
            hidden = xv[block, :].astype(F32)
            scale = lax.rsqrt(jnp.sum(hidden * hidden, axis=1, keepdims=True) / hidden.shape[1] + 1e-6)
            hidden = (hidden * scale).astype(BF16)
            for g in range(4):
                normed[g, block, :] = hidden[:, g * 1280:(g + 1) * 1280]
            return carry

        lax.fori_loop(0, rows // 16, norm_rows, 0, unroll=3)

    seen = []

    def query_product(x):
        q_swap.done(x)
        where = place.shifted("x", x)
        product = dot(normed[where], wq[pl.ds(where * 4, 4)].reshape(1280, 640))
        if seen:
            qacc[...] += product
        else:
            qacc[...] = product
        seen.append(x)

    def finish_queries():
        scaled = (qacc[...] * factor).astype(BF16)
        for h in range(heads):
            queries[h] = scaled[:, h * 128:(h + 1) * 128]
        top[...] = jnp.full_like(top, LOW)
        accum[...] = jnp.zeros_like(accum)

    def handed(batch):
        copies.arrived(("kv swap", batch), kv.at[pl.ds(0, 4 if batch == 1 else 2)])

    def attend(k, c):
        part = place.shifted("y", k)
        lane = lax.broadcasted_iota(jnp.int32, (1, 16 * PART), 1)
        chip = jnp.zeros_like(lane)
        for n in range(1, 16):
            chip = chip + (lane >= n * PART).astype(jnp.int32)
        position = chip * (2 * rows - PART) + lane + (c * rows + part * PART)
        row = lax.broadcasted_iota(jnp.int32, (rows, 1), 0) + ctx * rows
        bias = jnp.where(position <= row, 0.0, NEG)
        keys = kv[group(0, part, c)].reshape(16 * PART, 128)
        values = kv[group(1, part, c)].reshape(16 * PART, 128)
        both = jnp.concatenate([values, jnp.ones((16 * PART, 128), BF16)], axis=1)
        for h in range(heads):
            scores = dot(queries[h], keys, NT) + bias
            old = top[h]
            new = jnp.maximum(old, spread(jnp.max(scores, axis=1, keepdims=True), 128))
            expo = jnp.exp(scores - jnp.tile(new, (1, 6)))
            fade = jnp.exp(old - new)
            accum[h] = accum[h] * jnp.tile(fade, (1, 2)) + dot(expo.astype(BF16), both)
            top[h] = new

    def finish_cross():
        for h in range(heads):
            cross[:, h * 128:(h + 1) * 128] = (accum[h, :, 0:128] / accum[h, :, 128:256]).astype(BF16)
        for k in range(4):
            shared[k * PART:(k + 1) * PART, 0:128] = kv[group(0, k, core), me]
            shared[k * PART:(k + 1) * PART, 128:256] = kv[group(1, k, core), me]

    def update(x):
        o_swap.done(x)
        where = place.shifted("x", x)
        for pair in range(2):
            w = wo[pl.ds(where * 4 + 2 * pair, 2)].reshape(640, 640)
            slot = (x % 4) * 2 + pair
            res[slot] = dot(cross[...], w, NT).astype(BF16)
            block = pl.ds(pl.multiple_of((where * 2 + pair) * 640, 640), 640)
            copies.local(res.at[slot], out.at[0, :, block], "out")

    start()
    copies.left("wo in", wo.at[me, core])
    oa.start2(0)
    qa.start2(0)
    qb.start1()
    normalise()
    ob.start1()
    qb.start2(0)
    oa.forward2(0)
    qa.start1()
    self_x()
    window_attention()
    qb.forward1()
    qa.forward2(0)
    ob.forward1()
    oa.finish2(0)
    o_swap.far(0)
    qb.forward2(0)
    qb.start2(1)
    qb.start2(-1)
    qa.forward1()
    qa.start2(1)
    qa.start2(-1)
    qb.finish2(0)
    q_swap.rest(0)
    self_swap()
    mix()
    qa.finish2(0)
    q_swap.far(0)
    qb.forward2(1)
    qb.forward2(-1)
    qb.start2(2)
    qa.forward2(1)
    reduce()
    qb.finish2(1)
    q_swap.rest(1)
    qa.start2(2)
    q_swap.most(0)
    qb.finish2(-1)
    q_swap.rest(-1)
    oa.start1()
    query_product(0)
    qa.finish2(1)
    q_swap.far(1)
    kv_x()
    qa.forward2(-1)
    qa.forward2(2)
    q_swap.most(-1)
    q_swap.most(1)
    qb.forward2(2)
    query_product(-1)
    kv_round()
    ob.start2(0)
    query_product(1)
    qa.finish2(-1)
    q_swap.far(-1)
    oa.forward1()
    oa.start2(1)
    oa.start2(-1)
    qb.finish2(2)
    q_swap.rest(2)
    qa.finish2(2)
    q_swap.far(2)
    query_product(2)
    finish_queries()
    kv_across()
    attend(0, core)
    handed(0)
    attend(0, 1 - core)
    round_forward(half)
    ob.start2(-1)
    ob.forward2(0)
    oa.forward2(1)
    ob.start2(1)
    oa.start2(2)
    o_swap.most(0)
    ob.start2(2)
    oa.forward2(-1)
    round_forward(other)
    attend(-1, core)
    ob.forward2(-1)
    handed(1)
    attend(-1, 1 - core)
    oa.finish2(1)
    ob.finish2(0)
    o_swap.far(1)
    round_end(half)
    o_swap.rest(0)
    attend(1, 1 - core)
    round_end(other)
    ob.forward2(1)
    attend(2, core)
    ob.forward2(2)
    oa.forward2(2)
    handed(2)
    attend(2, 1 - core)
    ob.finish2(-1)
    o_swap.rest(-1)
    o_swap.most(-1)
    o_swap.most(1)
    oa.finish2(-1)
    o_swap.far(-1)
    attend(1, core)
    ob.finish2(1)
    o_swap.rest(1)
    finish_cross()
    ob.finish2(2)
    o_swap.rest(2)
    update(0)
    oa.finish2(2)
    o_swap.far(2)
    update(-1)
    update(1)
    update(2)

    for gather in (qa, qb, oa, ob):
        gather.sent()
    copies.left(("wq", "swap"), wq.at[:, 0])
    copies.left(("wo", "swap"), wo.at[:, 0])
    copies.left("self z", sz.at[pl.ds(0, 3)])
    copies.left("self x", sw.at[pl.ds(0, 3), 0])
    copies.left("self swap", sw.at[:, 0])
    copies.left("rim", near.at[pl.ds(0, 128)])
    copies.left("reduce", gathered)
    copies.left("kv piece", kv.at[0, pl.ds(0, 15)])
    copies.left("kv group", kv.at[pl.ds(0, 7)])
    copies.left("kv swap", kv.at[pl.ds(0, 8)])
    copies.left("out", res)
    assert (len(copies.sends), len(copies.recvs)) == (SENDS, RECVS), (len(copies.sends), len(copies.recvs))


SENDS = 22
RECVS = 63


def per_device(layer_input, self_q, self_kv, self_out_weight, kv_weight, q_weight, out_weight):
    vmem = pl.BlockSpec(memory_space=pltpu.VMEM)
    hbm = pl.BlockSpec(memory_space=pltpu.HBM)
    free = pl.BlockSpec(memory_space=pl.ANY)
    tokens = self_q.shape[0]
    columns = kv_weight.shape[0]
    arrays = (layer_input, self_q, self_kv, self_out_weight.T, kv_weight, q_weight, out_weight[0].T)
    return pl.pallas_call(
        kernel,
        name="layer_group",
        out_shape=(jax.ShapeDtypeStruct((1, tokens, 5120), BF16), jax.ShapeDtypeStruct((tokens, 256), BF16)),
        in_specs=[hbm] * 7,
        out_specs=(free, vmem),
        scratch_shapes=[
            pltpu.VMEM((tokens, 640), BF16),
            pltpu.VMEM((columns, 640), BF16),
            pltpu.VMEM((columns, 256), BF16),
            pltpu.VMEM((tokens, 5120), BF16),
            pltpu.VMEM((4, tokens, 1280), BF16),
            pltpu.VMEM((16, 2, 160, 640), BF16),
            pltpu.VMEM((16, 2, 160, 640), BF16),
            pltpu.VMEM((4, SELF_ROWS, 896), BF16),
            pltpu.VMEM((4, 2, 4 * columns, 896), BF16),
            pltpu.VMEM((320, 256), BF16),
            pltpu.VMEM((16, 16, PART, 128), BF16),
            pltpu.VMEM((8, PART + 8, 128), F32),
            pltpu.VMEM((7, PART + 8, 128), F32),
            pltpu.VMEM((tokens, 640), BF16),
            pltpu.VMEM((tokens, 640), F32),
            pltpu.VMEM((5, tokens, 128), BF16),
            pltpu.VMEM((5, tokens, 128), F32),
            pltpu.VMEM((5, tokens, 256), F32),
            pltpu.VMEM((tokens, 640), BF16),
            pltpu.VMEM((8, tokens, 640), BF16),
            pltpu.SemaphoreType.DMA((SENDS,)),
            pltpu.SemaphoreType.DMA((RECVS,)),
        ],
        compiler_params=pltpu.CompilerParams(
            collective_id=0, has_side_effects=True, vmem_limit_bytes=36 << 20),
    )(*[pltpu.with_memory_space_constraint(array, pltpu.HBM) for array in arrays])


def solution(mesh):
    return jax.shard_map(
        per_device,
        mesh=mesh,
        in_specs=(
            P("section", "ctx", None),
            P("ctx", None),
            P("ctx", None),
            P(None, ("section", "ctx")),
            P(("section", "ctx"), None),
            P("section", "ctx", None),
            P("section", None, "ctx"),
        ),
        out_specs=(P("section", "ctx", None), P("ctx", None)),
        check_vma=False,
    )
```

```python
import functools
import math

import jax
import jax.numpy as jnp
from jax import lax
from jax.experimental import pallas as pl
from jax.experimental.pallas import tpu as pltpu
from jax.sharding import PartitionSpec as P

MESH = pl.DeviceIdType.MESH
WINDOW = 128
F32 = jnp.float32
BF16 = jnp.bfloat16
NEG = -1e30

NT = (((1,), (1,)), ((), ()))
NN = (((1,), (0,)), ((), ()))

PART = 48
LOW = -1e20


def dot(a, b, dims=NN):
    return lax.dot_general(a, b, dims, preferred_element_type=F32)


class Place:
    def __init__(self):
        section = lax.axis_index("section")
        ctx = lax.axis_index("ctx")
        self.at = dict(zl=section // 4, y=section % 4, x=ctx // 8, zh=(ctx // 2) % 4, co=ctx % 2)
        self.ctx = ctx
        self.section = section

    SIZE = dict(zl=2, y=4, x=4, zh=4, co=2)

    def shifted(self, axis, step):
        size = self.SIZE[axis]
        return lax.rem(self.at[axis] + (step + size), size)

    def device(self, **steps):
        c = dict(self.at)
        for axis, step in steps.items():
            c[axis] = self.shifted(axis, step)
        return (c["zl"] * 4 + c["y"], (c["x"] * 4 + c["zh"]) * 2 + c["co"])

    def ctx_device(self, step):
        return (self.section, lax.rem(self.ctx + step + 32, 32))


class Copies:
    def __init__(self, send, recv):
        self.send, self.recv = send, recv
        self.sends, self.recvs = {}, {}

    def index(self, table, name):
        return table.setdefault(name, len(table))

    def remote(self, ref, device, send, recv, dst=None):
        pltpu.make_async_remote_copy(
            src_ref=ref, dst_ref=ref if dst is None else dst,
            send_sem=self.send.at[self.index(self.sends, send)],
            recv_sem=self.recv.at[self.index(self.recvs, recv)],
            device_id=device, device_id_type=MESH).start()

    def local(self, src, dst, send):
        pltpu.make_async_copy(src, dst, self.send.at[self.index(self.sends, send)]).start()

    def arrived(self, recv, like):
        pltpu.make_async_copy(like, like, self.recv.at[self.recvs[recv]]).wait()

    def left(self, send, like):
        pltpu.make_async_copy(like, like, self.send.at[self.sends[send]]).wait()


class Gather:
    def __init__(self, name, place, copies, buf, low, cut, high, first, second):
        self.name, self.place, self.copies, self.buf = name, place, copies, buf
        self.low, self.cut, self.high = low, cut, high
        self.first, self.second = first, second

    def put(self, key, i, j, low, high, axis, step):
        x, zh = (i, j) if self.first == "x" else (j, i)
        index = self.place.shifted("x", x) * 4 + self.place.shifted("zh", zh)
        ref = self.buf.at[index, self.place.at["co"], pl.ds(low, high - low)]
        self.copies.remote(ref, self.place.device(**{axis: step}), self.name, (self.name, key))

    def like(self, blocks):
        return self.buf.at[pl.ds(0, blocks), 0, pl.ds(self.low, self.high - self.low)]

    def got(self, key, blocks):
        self.copies.arrived((self.name, key), self.like(blocks))

    def start1(self):
        self.put("near", 0, 0, self.low, self.high, self.first, 1)
        self.put("near", 0, 0, self.low, self.high, self.first, -1)

    def forward1(self):
        self.got("near", 2)
        self.put("far", -1, 0, self.low, self.cut, self.first, 1)
        self.put("far", 1, 0, self.cut, self.high, self.first, -1)

    def start2(self, i):
        if i == 2:
            self.got("far", 1)
        self.put(("near", i), i, 0, self.low, self.high, self.second, 1)
        self.put(("near", i), i, 0, self.low, self.high, self.second, -1)

    def forward2(self, i):
        self.got(("near", i), 2)
        self.put(("far", i), i, -1, self.low, self.cut, self.second, 1)
        self.put(("far", i), i, 1, self.cut, self.high, self.second, -1)

    def finish2(self, i):
        self.got(("far", i), 1)

    def sent(self):
        self.copies.left(self.name, self.like(15))


class Swap:
    def __init__(self, name, place, copies, buf):
        self.name, self.place, self.copies, self.buf = name, place, copies, buf

    def put(self, x, ref):
        self.copies.remote(ref, self.place.device(co=1), (self.name, "swap"), (self.name, "swap", x))

    def rows(self, x, low, count):
        return self.buf.at[pl.ds(self.place.shifted("x", x) * 4, 4), self.place.at["co"], pl.ds(low, count)]

    def most(self, x):
        self.put(x, self.rows(x, 0, 128))

    def far(self, i):
        index = self.place.shifted("x", 2) * 4 + self.place.shifted("zh", i)
        self.put(2, self.buf.at[index, self.place.at["co"], pl.ds(0, 128)])

    def rest(self, x):
        self.put(x, self.rows(x, 128, 32))

    def done(self, x):
        self.copies.arrived((self.name, "swap", x), self.buf.at[pl.ds(0, 4), 0])


def eye_rows(rows, columns):
    return lax.broadcasted_iota(jnp.int32, (rows, columns), 0) == lax.broadcasted_iota(jnp.int32, (rows, columns), 1)


def spread(column, width):
    return jnp.broadcast_to(column, (column.shape[0], width))


def kernel(x_in, q_hbm, kv_in, so_hbm, kw_hbm, wq_in, wo_in, out, shared,
           q_in, so_in, kw_in, xv, normed, wq, wo, sz, sw, near, kv, stage, gathered, window, qacc, queries, top, accum, cross, res,
           send, recv):
    place = Place()
    copies = Copies(send, recv)
    ctx = place.ctx
    at = place.at
    me = at["x"] * 4 + at["zh"]
    core = at["co"]
    rows = q_in.shape[0]
    heads = q_in.shape[1] // 128
    factor = 1.0 / math.sqrt(128)
    sibling = place.device(co=1)
    columns = so_in.shape[0]

    friends = [place.device(x=1), place.device(x=-1), place.device(x=2), place.device(zh=1), place.device(zh=-1),
               place.device(zh=2), sibling, place.ctx_device(1), place.ctx_device(-1)]
    for zl in (0, 1):
        for y in range(4):
            if zl or y:
                friends.append(place.device(zl=zl, y=y))
    barrier = pltpu.get_barrier_semaphore()
    for friend in friends:
        pl.semaphore_signal(barrier, inc=1, device_id=friend, device_id_type=MESH)

    copies.local(so_hbm, so_in, "so in")
    copies.local(kw_hbm, kw_in, "kw in")
    copies.local(kv_in, near.at[pl.ds(128, rows)], "kv in")
    copies.local(wq_in.at[0], wq.at[me, core], "wq in")
    copies.local(q_hbm, q_in, "q in")
    copies.local(x_in.at[0], xv, "x in")
    copies.local(wo_in, wo.at[me, core], "wo in")

    sz[at["zh"], 112:144, :] = jnp.zeros((32, 128), BF16)
    copies.left("so in", so_in)
    copies.left("kw in", kw_in)
    for n in range(7):
        ref, lane = (so_in, n * 128) if n < 5 else (kw_in, (n - 5) * 128)
        sz[at["zh"], 16 * n:16 * n + 16, :] = ref[0:16, lane:lane + 128]
        sz[at["zh"], 112 + 4 * n:116 + 4 * n, :] = ref[16:20, lane:lane + 128]
    copies.left("kv in", near.at[pl.ds(128, rows)])
    copies.left("wq in", wq.at[me, core])
    pl.semaphore_wait(barrier, len(friends))

    qa = Gather("qa", place, copies, wq, 0, 64, 128, "zh", "x")
    qb = Gather("qb", place, copies, wq, 128, 144, 160, "x", "zh")
    oa = Gather("oa", place, copies, wo, 0, 64, 128, "zh", "x")
    ob = Gather("ob", place, copies, wo, 128, 144, 160, "x", "zh")
    half, y = at["zl"], at["y"]
    other = lax.rem(half + 1, 2)
    diagonal = eye_rows(PART, 128)

    def group(h, part, c):
        return (h * 4 + part) * 2 + c

    mine = group(half, y, core)

    q_swap = Swap("wq", place, copies, wq)
    o_swap = Swap("wo", place, copies, wo)

    def start():
        for k in (1, -1, 2):
            copies.remote(sz.at[at["zh"]], place.device(zh=k), "self z", "self z")
        copies.remote(near.at[pl.ds(192, 128)], place.ctx_device(1), "rim", "rim", near.at[pl.ds(0, 128)])

    def window_attention():
        copies.left("q in", q_in)
        copies.arrived("rim", near.at[pl.ds(0, 128)])
        qpos = lax.broadcasted_iota(jnp.int32, (rows, 320), 0)
        kpos = lax.broadcasted_iota(jnp.int32, (rows, 320), 1) - 128
        allowed = (kpos <= qpos) & (kpos > qpos - WINDOW) & (kpos >= -rows * ctx)
        for h in range(heads):
            scores = dot(q_in[:, h * 128:(h + 1) * 128], near[:, 0:128], NT) * factor
            scores = jnp.where(allowed, scores, NEG)
            expo = jnp.exp(scores - jnp.max(scores, axis=1, keepdims=True))
            numer = dot(expo.astype(BF16), near[:, 128:256])
            window[:, h * 128:(h + 1) * 128] = (numer / jnp.sum(expo, axis=1, keepdims=True)).astype(BF16)

    def self_x():
        copies.arrived("self z", sz.at[pl.ds(0, 3)])
        for k in range(4):
            for n in range(7):
                lanes = slice(n * 128, n * 128 + 128)
                sw[at["x"], core, k * 20:k * 20 + 16, lanes] = sz[k, 16 * n:16 * n + 16, :]
                sw[at["x"], core, k * 20 + 16:k * 20 + 20, lanes] = sz[k, 112 + 4 * n:116 + 4 * n, :]
        own = sw.at[at["x"], core]
        for k in (1, -1, 2):
            copies.remote(own, place.device(x=k), "self x", "self x")
        copies.remote(own, sibling, "self swap", "self swap")

    def self_swap():
        copies.arrived("self x", sw.at[pl.ds(0, 3), 0])
        for k in (1, -1, 2):
            copies.remote(sw.at[place.shifted("x", k), core], sibling, "self swap", "self swap")

    def mix():
        copies.arrived("self swap", sw.at[:, 0])
        weights = sw[...].reshape(32 * columns, 896)
        mixed = dot(window[...], weights[:, 0:640], NT).astype(BF16)
        wide = mixed.astype(F32)
        squares = jnp.sum(wide * wide, axis=1, keepdims=True)
        raw = dot(mixed, weights[:, 640:896])
        for s in range(8):
            part, side = s % 4, s // 4
            stage[s, 0:PART] = raw[part * PART:(part + 1) * PART, side * 128:(side + 1) * 128]
            line = jnp.sum(jnp.where(diagonal, squares[part * PART:(part + 1) * PART], 0.0), axis=0, keepdims=True)
            stage[s, PART:PART + 8] = jnp.broadcast_to(line, (8, 128))
        for zl in (0, 1):
            for k in range(4):
                if zl or k:
                    to = place.device(zl=zl, y=k)
                    copies.remote(stage.at[to[0]], to, "reduce", "reduce", gathered.at[zl * 4 + k - 1])

    def reduce():
        copies.arrived("reduce", gathered)
        summed = stage[place.section]
        for slot in range(7):
            summed = summed + gathered[slot]
        column = jnp.sum(jnp.where(diagonal, summed[PART:PART + 1], 0.0), axis=1, keepdims=True)
        kv[mine, me] = (summed[0:PART] * lax.rsqrt(column / 5120.0 + 1e-6)).astype(BF16)
        for k in (1, -1, 2):
            copies.remote(kv.at[mine, me], place.device(zh=k), "kv piece", "kv z")

    def kv_x():
        copies.arrived("kv z", kv.at[0, pl.ds(0, 3)])
        for k in (1, -1, 2):
            copies.remote(kv.at[mine, pl.ds(at["x"] * 4, 4)], place.device(x=k), "kv piece", "kv x")

    def round_start(h):
        for k in (1, -1):
            copies.remote(kv.at[group(h, y, core)], place.device(y=k), "kv group", ("kv near", h is half))

    def hand(h, part, batch):
        copies.remote(kv.at[group(h, part, core)], sibling, "kv swap", ("kv swap", batch))

    def kv_round():
        copies.arrived("kv x", kv.at[0, pl.ds(0, 12)])
        copies.remote(kv.at[mine], place.device(zl=1), "kv group", "kv across")
        round_start(half)
        hand(half, y, 0)

    def kv_across():
        copies.arrived("kv across", kv.at[0])
        round_start(other)
        hand(other, y, 0)

    def round_forward(h):
        copies.arrived(("kv near", h is half), kv.at[pl.ds(0, 2)])
        copies.remote(kv.at[group(h, place.shifted("y", -1), core), pl.ds(0, 8)], place.device(y=1),
                      "kv group", ("kv far", h is half))
        copies.remote(kv.at[group(h, place.shifted("y", 1), core), pl.ds(8, 8)], place.device(y=-1),
                      "kv group", ("kv far", h is half))
        for k in (1, -1):
            hand(h, place.shifted("y", k), 1)

    def round_end(h):
        copies.arrived(("kv far", h is half), kv.at[0])
        hand(h, place.shifted("y", 2), 2)

    def normalise():
        copies.left("x in", xv)

        def norm_rows(i, carry):
            block = pl.ds(pl.multiple_of(i * 16, 16), 16)
            hidden = xv[block, :].astype(F32)
            scale = lax.rsqrt(jnp.sum(hidden * hidden, axis=1, keepdims=True) / hidden.shape[1] + 1e-6)
            hidden = (hidden * scale).astype(BF16)
            for g in range(4):
                normed[g, block, :] = hidden[:, g * 1280:(g + 1) * 1280]
            return carry

        lax.fori_loop(0, rows // 16, norm_rows, 0, unroll=3)

    seen = []

    def query_product(x):
        q_swap.done(x)
        where = place.shifted("x", x)
        product = dot(normed[where], wq[pl.ds(where * 4, 4)].reshape(1280, 640))
        if seen:
            qacc[...] += product
        else:
            qacc[...] = product
        seen.append(x)

    def finish_queries():
        scaled = (qacc[...] * factor).astype(BF16)
        for h in range(heads):
            queries[h] = scaled[:, h * 128:(h + 1) * 128]
        top[...] = jnp.full_like(top, LOW)
        accum[...] = jnp.zeros_like(accum)

    def handed(batch):
        copies.arrived(("kv swap", batch), kv.at[pl.ds(0, 4 if batch == 1 else 2)])

    def attend(k, c):
        part = place.shifted("y", k)
        lane = lax.broadcasted_iota(jnp.int32, (1, 16 * PART), 1)
        chip = jnp.zeros_like(lane)
        for n in range(1, 16):
            chip = chip + (lane >= n * PART).astype(jnp.int32)
        position = chip * (2 * rows - PART) + lane + (c * rows + part * PART)
        row = lax.broadcasted_iota(jnp.int32, (rows, 1), 0) + ctx * rows
        bias = jnp.where(position <= row, 0.0, NEG)
        keys = kv[group(0, part, c)].reshape(16 * PART, 128)
        values = kv[group(1, part, c)].reshape(16 * PART, 128)
        both = jnp.concatenate([values, jnp.ones((16 * PART, 128), BF16)], axis=1)
        for h in range(heads):
            scores = dot(queries[h], keys, NT) + bias
            old = top[h]
            new = jnp.maximum(old, spread(jnp.max(scores, axis=1, keepdims=True), 128))
            expo = jnp.exp(scores - jnp.tile(new, (1, 6)))
            fade = jnp.exp(old - new)
            accum[h] = accum[h] * jnp.tile(fade, (1, 2)) + dot(expo.astype(BF16), both)
            top[h] = new

    def finish_cross():
        for h in range(heads):
            cross[:, h * 128:(h + 1) * 128] = (accum[h, :, 0:128] / accum[h, :, 128:256]).astype(BF16)
        for k in range(4):
            shared[k * PART:(k + 1) * PART, 0:128] = kv[group(0, k, core), me]
            shared[k * PART:(k + 1) * PART, 128:256] = kv[group(1, k, core), me]

    def update(x):
        o_swap.done(x)
        where = place.shifted("x", x)
        for pair in range(2):
            w = wo[pl.ds(where * 4 + 2 * pair, 2)].reshape(640, 640)
            slot = (x % 4) * 2 + pair
            res[slot] = dot(cross[...], w, NT).astype(BF16)
            block = pl.ds(pl.multiple_of((where * 2 + pair) * 640, 640), 640)
            copies.local(res.at[slot], out.at[0, :, block], "out")

    start()
    copies.left("wo in", wo.at[me, core])
    oa.start2(0)
    qa.start2(0)
    qb.start1()
    normalise()
    ob.start1()
    qa.start1()
    self_x()
    oa.forward2(0)
    window_attention()
    qa.forward2(0)
    qb.forward1()
    qb.start2(-1)
    ob.forward1()
    qb.start2(0)
    qb.start2(1)
    qb.forward2(-1)
    qa.forward1()
    self_swap()
    qa.start2(-1)
    qa.start2(1)
    mix()
    qb.finish2(-1)
    q_swap.rest(-1)
    oa.finish2(0)
    o_swap.far(0)
    qa.finish2(0)
    q_swap.far(0)
    qb.forward2(1)
    qb.forward2(0)
    qb.start2(2)
    qa.start2(2)
    q_swap.most(0)
    reduce()
    qb.finish2(1)
    q_swap.rest(1)
    qb.finish2(0)
    q_swap.rest(0)
    oa.start1()
    query_product(0)
    qa.forward2(-1)
    kv_x()
    qa.forward2(1)
    qa.forward2(2)
    q_swap.most(-1)
    q_swap.most(1)
    qb.forward2(2)
    qa.finish2(-1)
    q_swap.far(-1)
    query_product(-1)
    ob.start2(0)
    query_product(1)
    kv_round()
    oa.forward1()
    oa.start2(-1)
    oa.start2(1)
    qb.finish2(2)
    q_swap.rest(2)
    qa.finish2(1)
    q_swap.far(1)
    qa.finish2(2)
    q_swap.far(2)
    ob.start2(-1)
    query_product(2)
    finish_queries()
    kv_across()
    attend(0, core)
    handed(0)
    attend(0, 1 - core)
    oa.forward2(-1)
    round_forward(half)
    ob.forward2(0)
    oa.start2(2)
    o_swap.most(0)
    ob.start2(1)
    ob.start2(2)
    oa.forward2(1)
    ob.forward2(-1)
    round_forward(other)
    attend(1, core)
    ob.finish2(0)
    o_swap.rest(0)
    oa.finish2(-1)
    o_swap.far(-1)
    handed(1)
    attend(-1, 1 - core)
    ob.forward2(1)
    round_end(half)
    attend(1, 1 - core)
    round_end(other)
    ob.forward2(2)
    oa.forward2(2)
    ob.finish2(-1)
    o_swap.rest(-1)
    attend(2, core)
    handed(2)
    attend(2, 1 - core)
    ob.finish2(1)
    o_swap.rest(1)
    oa.finish2(1)
    o_swap.far(1)
    o_swap.most(1)
    o_swap.most(-1)
    attend(-1, core)
    ob.finish2(2)
    o_swap.rest(2)
    finish_cross()
    update(0)
    oa.finish2(2)
    o_swap.far(2)
    update(1)
    update(-1)
    update(2)

    for gather in (qa, qb, oa, ob):
        gather.sent()
    copies.left(("wq", "swap"), wq.at[:, 0])
    copies.left(("wo", "swap"), wo.at[:, 0])
    copies.left("self z", sz.at[pl.ds(0, 3)])
    copies.left("self x", sw.at[pl.ds(0, 3), 0])
    copies.left("self swap", sw.at[:, 0])
    copies.left("rim", near.at[pl.ds(0, 128)])
    copies.left("reduce", gathered)
    copies.left("kv piece", kv.at[0, pl.ds(0, 15)])
    copies.left("kv group", kv.at[pl.ds(0, 7)])
    copies.left("kv swap", kv.at[pl.ds(0, 8)])
    copies.left("out", res)
    assert (len(copies.sends), len(copies.recvs)) == (SENDS, RECVS), (len(copies.sends), len(copies.recvs))


SENDS = 22
RECVS = 63


def per_device(layer_input, self_q, self_kv, self_out_weight, kv_weight, q_weight, out_weight):
    vmem = pl.BlockSpec(memory_space=pltpu.VMEM)
    hbm = pl.BlockSpec(memory_space=pltpu.HBM)
    free = pl.BlockSpec(memory_space=pl.ANY)
    tokens = self_q.shape[0]
    columns = kv_weight.shape[0]
    arrays = (layer_input, self_q, self_kv, self_out_weight.T, kv_weight, q_weight, out_weight[0].T)
    return pl.pallas_call(
        kernel,
        name="layer_group",
        out_shape=(jax.ShapeDtypeStruct((1, tokens, 5120), BF16), jax.ShapeDtypeStruct((tokens, 256), BF16)),
        in_specs=[hbm] * 7,
        out_specs=(free, vmem),
        scratch_shapes=[
            pltpu.VMEM((tokens, 640), BF16),
            pltpu.VMEM((columns, 640), BF16),
            pltpu.VMEM((columns, 256), BF16),
            pltpu.VMEM((tokens, 5120), BF16),
            pltpu.VMEM((4, tokens, 1280), BF16),
            pltpu.VMEM((16, 2, 160, 640), BF16),
            pltpu.VMEM((16, 2, 160, 640), BF16),
            pltpu.VMEM((4, 144, 128), BF16),
            pltpu.VMEM((4, 2, 4 * columns, 896), BF16),
            pltpu.VMEM((320, 256), BF16),
            pltpu.VMEM((16, 16, PART, 128), BF16),
            pltpu.VMEM((8, PART + 8, 128), F32),
            pltpu.VMEM((7, PART + 8, 128), F32),
            pltpu.VMEM((tokens, 640), BF16),
            pltpu.VMEM((tokens, 640), F32),
            pltpu.VMEM((5, tokens, 128), BF16),
            pltpu.VMEM((5, tokens, 128), F32),
            pltpu.VMEM((5, tokens, 256), F32),
            pltpu.VMEM((tokens, 640), BF16),
            pltpu.VMEM((8, tokens, 640), BF16),
            pltpu.SemaphoreType.DMA((SENDS,)),
            pltpu.SemaphoreType.DMA((RECVS,)),
        ],
        compiler_params=pltpu.CompilerParams(
            collective_id=0, has_side_effects=True, vmem_limit_bytes=36 << 20),
    )(*[pltpu.with_memory_space_constraint(array, pltpu.HBM) for array in arrays])


def solution(mesh):
    return jax.shard_map(
        per_device,
        mesh=mesh,
        in_specs=(
            P("section", "ctx", None),
            P("ctx", None),
            P("ctx", None),
            P(None, ("section", "ctx")),
            P(("section", "ctx"), None),
            P("section", "ctx", None),
            P("section", None, "ctx"),
        ),
        out_specs=(P("section", "ctx", None), P("ctx", None)),
        check_vma=False,
    )
```

```python
import functools
import math

import jax
import jax.numpy as jnp
from jax import lax
from jax.experimental import pallas as pl
from jax.experimental.pallas import tpu as pltpu
from jax.sharding import PartitionSpec as P

MESH = pl.DeviceIdType.MESH
WINDOW = 128
F32 = jnp.float32
BF16 = jnp.bfloat16
NEG = -1e30

NT = (((1,), (1,)), ((), ()))
NN = (((1,), (0,)), ((), ()))

PART = 48
LOW = -1e20


def dot(a, b, dims=NN):
    return lax.dot_general(a, b, dims, preferred_element_type=F32)


class Place:
    def __init__(self):
        section = lax.axis_index("section")
        ctx = lax.axis_index("ctx")
        self.at = dict(zl=section // 4, y=section % 4, x=ctx // 8, zh=(ctx // 2) % 4, co=ctx % 2)
        self.ctx = ctx
        self.section = section

    SIZE = dict(zl=2, y=4, x=4, zh=4, co=2)

    def shifted(self, axis, step):
        size = self.SIZE[axis]
        return lax.rem(self.at[axis] + (step + size), size)

    def device(self, **steps):
        c = dict(self.at)
        for axis, step in steps.items():
            c[axis] = self.shifted(axis, step)
        return (c["zl"] * 4 + c["y"], (c["x"] * 4 + c["zh"]) * 2 + c["co"])

    def ctx_device(self, step):
        return (self.section, lax.rem(self.ctx + step + 32, 32))


class Copies:
    def __init__(self, send, recv):
        self.send, self.recv = send, recv
        self.sends, self.recvs = {}, {}

    def index(self, table, name):
        return table.setdefault(name, len(table))

    def remote(self, ref, device, send, recv, dst=None):
        pltpu.make_async_remote_copy(
            src_ref=ref, dst_ref=ref if dst is None else dst,
            send_sem=self.send.at[self.index(self.sends, send)],
            recv_sem=self.recv.at[self.index(self.recvs, recv)],
            device_id=device, device_id_type=MESH).start()

    def local(self, src, dst, send):
        pltpu.make_async_copy(src, dst, self.send.at[self.index(self.sends, send)]).start()

    def arrived(self, recv, like):
        pltpu.make_async_copy(like, like, self.recv.at[self.recvs[recv]]).wait()

    def left(self, send, like):
        pltpu.make_async_copy(like, like, self.send.at[self.sends[send]]).wait()


class Gather:
    def __init__(self, name, place, copies, buf, low, cut, high, first, second):
        self.name, self.place, self.copies, self.buf = name, place, copies, buf
        self.low, self.cut, self.high = low, cut, high
        self.first, self.second = first, second

    def put(self, key, i, j, low, high, axis, step):
        x, zh = (i, j) if self.first == "x" else (j, i)
        index = self.place.shifted("x", x) * 4 + self.place.shifted("zh", zh)
        ref = self.buf.at[index, self.place.at["co"], pl.ds(low, high - low)]
        self.copies.remote(ref, self.place.device(**{axis: step}), self.name, (self.name, key))

    def like(self, blocks):
        return self.buf.at[pl.ds(0, blocks), 0, pl.ds(self.low, self.high - self.low)]

    def got(self, key, blocks):
        self.copies.arrived((self.name, key), self.like(blocks))

    def start1(self):
        self.put("near", 0, 0, self.low, self.high, self.first, 1)
        self.put("near", 0, 0, self.low, self.high, self.first, -1)

    def forward1(self):
        self.got("near", 2)
        self.put("far", -1, 0, self.low, self.cut, self.first, 1)
        self.put("far", 1, 0, self.cut, self.high, self.first, -1)

    def start2(self, i):
        if i == 2:
            self.got("far", 1)
        self.put(("near", i), i, 0, self.low, self.high, self.second, 1)
        self.put(("near", i), i, 0, self.low, self.high, self.second, -1)

    def forward2(self, i):
        self.got(("near", i), 2)
        self.put(("far", i), i, -1, self.low, self.cut, self.second, 1)
        self.put(("far", i), i, 1, self.cut, self.high, self.second, -1)

    def finish2(self, i):
        self.got(("far", i), 1)

    def sent(self):
        self.copies.left(self.name, self.like(15))


class Swap:
    def __init__(self, name, place, copies, buf):
        self.name, self.place, self.copies, self.buf = name, place, copies, buf

    def put(self, x, ref):
        self.copies.remote(ref, self.place.device(co=1), (self.name, "swap"), (self.name, "swap", x))

    def rows(self, x, low, count):
        return self.buf.at[pl.ds(self.place.shifted("x", x) * 4, 4), self.place.at["co"], pl.ds(low, count)]

    def most(self, x):
        self.put(x, self.rows(x, 0, 128))

    def far(self, i):
        index = self.place.shifted("x", 2) * 4 + self.place.shifted("zh", i)
        self.put(2, self.buf.at[index, self.place.at["co"], pl.ds(0, 128)])

    def rest(self, x):
        self.put(x, self.rows(x, 128, 32))

    def done(self, x):
        self.copies.arrived((self.name, "swap", x), self.buf.at[pl.ds(0, 4), 0])


def eye_rows(rows, columns):
    return lax.broadcasted_iota(jnp.int32, (rows, columns), 0) == lax.broadcasted_iota(jnp.int32, (rows, columns), 1)


def spread(column, width):
    return jnp.broadcast_to(column, (column.shape[0], width))


def kernel(x_in, q_hbm, kv_in, so_in, kw_in, wq_in, wo_in, out, shared,
           q_in, xv, normed, wq, wo, sz, sw, near, kv, stage, gathered, window, qacc, queries, top, accum, cross, res,
           send, recv):
    place = Place()
    copies = Copies(send, recv)
    ctx = place.ctx
    at = place.at
    me = at["x"] * 4 + at["zh"]
    core = at["co"]
    rows = q_in.shape[0]
    heads = q_in.shape[1] // 128
    factor = 1.0 / math.sqrt(128)
    sibling = place.device(co=1)
    columns = so_in.shape[0]

    friends = [place.device(x=1), place.device(x=-1), place.device(x=2), place.device(zh=1), place.device(zh=-1),
               place.device(zh=2), sibling, place.ctx_device(1), place.ctx_device(-1)]
    for zl in (0, 1):
        for y in range(4):
            if zl or y:
                friends.append(place.device(zl=zl, y=y))
    barrier = pltpu.get_barrier_semaphore()
    for friend in friends:
        pl.semaphore_signal(barrier, inc=1, device_id=friend, device_id_type=MESH)

    copies.local(kv_in, near.at[pl.ds(128, rows)], "kv in")
    copies.local(wq_in.at[0], wq.at[me, core], "wq in")
    copies.local(q_hbm, q_in, "q in")
    copies.local(x_in.at[0], xv, "x in")
    copies.local(wo_in, wo.at[me, core], "wo in")

    sz[at["zh"], 112:144, :] = jnp.zeros((32, 128), BF16)
    for n in range(7):
        ref, lane = (so_in, n * 128) if n < 5 else (kw_in, (n - 5) * 128)
        sz[at["zh"], 16 * n:16 * n + 16, :] = ref[0:16, lane:lane + 128]
        sz[at["zh"], 112 + 4 * n:116 + 4 * n, :] = ref[16:20, lane:lane + 128]
    copies.left("kv in", near.at[pl.ds(128, rows)])
    copies.left("wq in", wq.at[me, core])
    pl.semaphore_wait(barrier, len(friends))

    qa = Gather("qa", place, copies, wq, 0, 64, 128, "zh", "x")
    qb = Gather("qb", place, copies, wq, 128, 144, 160, "x", "zh")
    oa = Gather("oa", place, copies, wo, 0, 64, 128, "zh", "x")
    ob = Gather("ob", place, copies, wo, 128, 144, 160, "x", "zh")
    half, y = at["zl"], at["y"]
    other = lax.rem(half + 1, 2)
    diagonal = eye_rows(PART, 128)

    def group(h, part, c):
        return (h * 4 + part) * 2 + c

    mine = group(half, y, core)

    q_swap = Swap("wq", place, copies, wq)
    o_swap = Swap("wo", place, copies, wo)

    def start():
        for k in (1, -1, 2):
            copies.remote(sz.at[at["zh"]], place.device(zh=k), "self z", "self z")
        copies.remote(near.at[pl.ds(192, 128)], place.ctx_device(1), "rim", "rim", near.at[pl.ds(0, 128)])

    def window_attention():
        copies.left("q in", q_in)
        copies.arrived("rim", near.at[pl.ds(0, 128)])
        qpos = lax.broadcasted_iota(jnp.int32, (rows, 320), 0)
        kpos = lax.broadcasted_iota(jnp.int32, (rows, 320), 1) - 128
        allowed = (kpos <= qpos) & (kpos > qpos - WINDOW) & (kpos >= -rows * ctx)
        for h in range(heads):
            scores = dot(q_in[:, h * 128:(h + 1) * 128], near[:, 0:128], NT) * factor
            scores = jnp.where(allowed, scores, NEG)
            expo = jnp.exp(scores - jnp.max(scores, axis=1, keepdims=True))
            numer = dot(expo.astype(BF16), near[:, 128:256])
            window[:, h * 128:(h + 1) * 128] = (numer / jnp.sum(expo, axis=1, keepdims=True)).astype(BF16)

    def self_x():
        copies.arrived("self z", sz.at[pl.ds(0, 3)])
        for k in range(4):
            for n in range(7):
                lanes = slice(n * 128, n * 128 + 128)
                sw[at["x"], core, k * 20:k * 20 + 16, lanes] = sz[k, 16 * n:16 * n + 16, :]
                sw[at["x"], core, k * 20 + 16:k * 20 + 20, lanes] = sz[k, 112 + 4 * n:116 + 4 * n, :]
        own = sw.at[at["x"], core]
        for k in (1, -1, 2):
            copies.remote(own, place.device(x=k), "self x", "self x")
        copies.remote(own, sibling, "self swap", "self swap")

    def self_swap():
        copies.arrived("self x", sw.at[pl.ds(0, 3), 0])
        for k in (1, -1, 2):
            copies.remote(sw.at[place.shifted("x", k), core], sibling, "self swap", "self swap")

    def mix():
        copies.arrived("self swap", sw.at[:, 0])
        weights = sw[...].reshape(32 * columns, 896)
        mixed = dot(window[...], weights[:, 0:640], NT).astype(BF16)
        wide = mixed.astype(F32)
        squares = jnp.sum(wide * wide, axis=1, keepdims=True)
        raw = dot(mixed, weights[:, 640:896])
        for s in range(8):
            part, side = s % 4, s // 4
            stage[s, 0:PART] = raw[part * PART:(part + 1) * PART, side * 128:(side + 1) * 128]
            line = jnp.sum(jnp.where(diagonal, squares[part * PART:(part + 1) * PART], 0.0), axis=0, keepdims=True)
            stage[s, PART:PART + 8] = jnp.broadcast_to(line, (8, 128))
        for zl in (0, 1):
            for k in range(4):
                if zl or k:
                    to = place.device(zl=zl, y=k)
                    copies.remote(stage.at[to[0]], to, "reduce", "reduce", gathered.at[zl * 4 + k - 1])

    def reduce():
        copies.arrived("reduce", gathered)
        summed = stage[place.section]
        for slot in range(7):
            summed = summed + gathered[slot]
        column = jnp.sum(jnp.where(diagonal, summed[PART:PART + 1], 0.0), axis=1, keepdims=True)
        kv[mine, me] = (summed[0:PART] * lax.rsqrt(column / 5120.0 + 1e-6)).astype(BF16)
        for k in (1, -1, 2):
            copies.remote(kv.at[mine, me], place.device(zh=k), "kv piece", "kv z")

    def kv_x():
        copies.arrived("kv z", kv.at[0, pl.ds(0, 3)])
        for k in (1, -1, 2):
            copies.remote(kv.at[mine, pl.ds(at["x"] * 4, 4)], place.device(x=k), "kv piece", "kv x")

    def round_start(h):
        for k in (1, -1):
            copies.remote(kv.at[group(h, y, core)], place.device(y=k), "kv group", ("kv near", h is half))

    def hand(h, part, batch):
        copies.remote(kv.at[group(h, part, core)], sibling, "kv swap", ("kv swap", batch))

    def kv_round():
        copies.arrived("kv x", kv.at[0, pl.ds(0, 12)])
        copies.remote(kv.at[mine], place.device(zl=1), "kv group", "kv across")
        round_start(half)
        hand(half, y, 0)

    def kv_across():
        copies.arrived("kv across", kv.at[0])
        round_start(other)
        hand(other, y, 0)

    def round_forward(h):
        copies.arrived(("kv near", h is half), kv.at[pl.ds(0, 2)])
        copies.remote(kv.at[group(h, place.shifted("y", -1), core), pl.ds(0, 8)], place.device(y=1),
                      "kv group", ("kv far", h is half))
        copies.remote(kv.at[group(h, place.shifted("y", 1), core), pl.ds(8, 8)], place.device(y=-1),
                      "kv group", ("kv far", h is half))
        for k in (1, -1):
            hand(h, place.shifted("y", k), 1)

    def round_end(h):
        copies.arrived(("kv far", h is half), kv.at[0])
        hand(h, place.shifted("y", 2), 2)

    def normalise():
        copies.left("x in", xv)

        def norm_rows(i, carry):
            block = pl.ds(pl.multiple_of(i * 16, 16), 16)
            hidden = xv[block, :].astype(F32)
            scale = lax.rsqrt(jnp.sum(hidden * hidden, axis=1, keepdims=True) / hidden.shape[1] + 1e-6)
            hidden = (hidden * scale).astype(BF16)
            for g in range(4):
                normed[g, block, :] = hidden[:, g * 1280:(g + 1) * 1280]
            return carry

        lax.fori_loop(0, rows // 16, norm_rows, 0, unroll=3)

    seen = []

    def query_product(x):
        q_swap.done(x)
        where = place.shifted("x", x)
        product = dot(normed[where], wq[pl.ds(where * 4, 4)].reshape(1280, 640))
        if seen:
            qacc[...] += product
        else:
            qacc[...] = product
        seen.append(x)

    def finish_queries():
        scaled = (qacc[...] * factor).astype(BF16)
        for h in range(heads):
            queries[h] = scaled[:, h * 128:(h + 1) * 128]
        top[...] = jnp.full_like(top, LOW)
        accum[...] = jnp.zeros_like(accum)

    def handed(batch):
        copies.arrived(("kv swap", batch), kv.at[pl.ds(0, 4 if batch == 1 else 2)])

    def attend(k, c):
        part = place.shifted("y", k)
        lane = lax.broadcasted_iota(jnp.int32, (1, 16 * PART), 1)
        chip = jnp.zeros_like(lane)
        for n in range(1, 16):
            chip = chip + (lane >= n * PART).astype(jnp.int32)
        position = chip * (2 * rows - PART) + lane + (c * rows + part * PART)
        row = lax.broadcasted_iota(jnp.int32, (rows, 1), 0) + ctx * rows
        bias = jnp.where(position <= row, 0.0, NEG)
        keys = kv[group(0, part, c)].reshape(16 * PART, 128)
        values = kv[group(1, part, c)].reshape(16 * PART, 128)
        both = jnp.concatenate([values, jnp.ones((16 * PART, 128), BF16)], axis=1)
        for h in range(heads):
            scores = dot(queries[h], keys, NT) + bias
            old = top[h]
            new = jnp.maximum(old, spread(jnp.max(scores, axis=1, keepdims=True), 128))
            expo = jnp.exp(scores - jnp.tile(new, (1, 6)))
            fade = jnp.exp(old - new)
            accum[h] = accum[h] * jnp.tile(fade, (1, 2)) + dot(expo.astype(BF16), both)
            top[h] = new

    def finish_cross():
        for h in range(heads):
            cross[:, h * 128:(h + 1) * 128] = (accum[h, :, 0:128] / accum[h, :, 128:256]).astype(BF16)
        for k in range(4):
            shared[k * PART:(k + 1) * PART, 0:128] = kv[group(0, k, core), me]
            shared[k * PART:(k + 1) * PART, 128:256] = kv[group(1, k, core), me]

    def update(x):
        o_swap.done(x)
        where = place.shifted("x", x)
        for pair in range(2):
            w = wo[pl.ds(where * 4 + 2 * pair, 2)].reshape(640, 640)
            slot = (x % 4) * 2 + pair
            res[slot] = dot(cross[...], w, NT).astype(BF16)
            block = pl.ds(pl.multiple_of((where * 2 + pair) * 640, 640), 640)
            copies.local(res.at[slot], out.at[0, :, block], "out")

    start()
    copies.left("wo in", wo.at[me, core])
    oa.start2(0)
    qa.start2(0)
    qb.start1()
    normalise()
    ob.start1()
    qa.start1()
    self_x()
    oa.forward2(0)
    window_attention()
    qa.forward2(0)
    qb.forward1()
    qb.start2(-1)
    ob.forward1()
    qb.start2(0)
    qb.start2(1)
    qb.forward2(-1)
    qa.forward1()
    self_swap()
    qa.start2(-1)
    qa.start2(1)
    mix()
    qb.finish2(-1)
    q_swap.rest(-1)
    oa.finish2(0)
    o_swap.far(0)
    qa.finish2(0)
    q_swap.far(0)
    qb.forward2(1)
    qb.forward2(0)
    qb.start2(2)
    qa.start2(2)
    q_swap.most(0)
    reduce()
    qb.finish2(1)
    q_swap.rest(1)
    qb.finish2(0)
    q_swap.rest(0)
    oa.start1()
    query_product(0)
    qa.forward2(-1)
    kv_x()
    qa.forward2(1)
    qa.forward2(2)
    q_swap.most(-1)
    q_swap.most(1)
    qb.forward2(2)
    qa.finish2(-1)
    q_swap.far(-1)
    query_product(-1)
    ob.start2(0)
    query_product(1)
    kv_round()
    oa.forward1()
    oa.start2(-1)
    oa.start2(1)
    qb.finish2(2)
    q_swap.rest(2)
    qa.finish2(1)
    q_swap.far(1)
    qa.finish2(2)
    q_swap.far(2)
    ob.start2(-1)
    query_product(2)
    finish_queries()
    kv_across()
    attend(0, core)
    handed(0)
    attend(0, 1 - core)
    oa.forward2(-1)
    round_forward(half)
    ob.forward2(0)
    oa.start2(2)
    o_swap.most(0)
    ob.start2(1)
    ob.start2(2)
    oa.forward2(1)
    ob.forward2(-1)
    round_forward(other)
    attend(1, core)
    ob.finish2(0)
    o_swap.rest(0)
    oa.finish2(-1)
    o_swap.far(-1)
    handed(1)
    attend(-1, 1 - core)
    ob.forward2(1)
    round_end(half)
    attend(1, 1 - core)
    round_end(other)
    ob.forward2(2)
    oa.forward2(2)
    ob.finish2(-1)
    o_swap.rest(-1)
    attend(2, core)
    handed(2)
    attend(2, 1 - core)
    ob.finish2(1)
    o_swap.rest(1)
    oa.finish2(1)
    o_swap.far(1)
    o_swap.most(1)
    o_swap.most(-1)
    attend(-1, core)
    ob.finish2(2)
    o_swap.rest(2)
    finish_cross()
    update(0)
    oa.finish2(2)
    o_swap.far(2)
    update(1)
    update(-1)
    update(2)

    for gather in (qa, qb, oa, ob):
        gather.sent()
    copies.left(("wq", "swap"), wq.at[:, 0])
    copies.left(("wo", "swap"), wo.at[:, 0])
    copies.left("self z", sz.at[pl.ds(0, 3)])
    copies.left("self x", sw.at[pl.ds(0, 3), 0])
    copies.left("self swap", sw.at[:, 0])
    copies.left("rim", near.at[pl.ds(0, 128)])
    copies.left("reduce", gathered)
    copies.left("kv piece", kv.at[0, pl.ds(0, 15)])
    copies.left("kv group", kv.at[pl.ds(0, 7)])
    copies.left("kv swap", kv.at[pl.ds(0, 8)])
    copies.left("out", res)
    assert (len(copies.sends), len(copies.recvs)) == (SENDS, RECVS), (len(copies.sends), len(copies.recvs))


SENDS = 20
RECVS = 63


def per_device(layer_input, self_q, self_kv, self_out_weight, kv_weight, q_weight, out_weight):
    vmem = pl.BlockSpec(memory_space=pltpu.VMEM)
    hbm = pl.BlockSpec(memory_space=pltpu.HBM)
    free = pl.BlockSpec(memory_space=pl.ANY)
    tokens = self_q.shape[0]
    columns = kv_weight.shape[0]
    arrays = (layer_input, self_q, self_kv, self_out_weight.T, kv_weight, q_weight, out_weight[0].T)
    return pl.pallas_call(
        kernel,
        name="layer_group",
        out_shape=(jax.ShapeDtypeStruct((1, tokens, 5120), BF16), jax.ShapeDtypeStruct((tokens, 256), BF16)),
        in_specs=[hbm, hbm, hbm, vmem, vmem, hbm, hbm],
        out_specs=(free, vmem),
        scratch_shapes=[
            pltpu.VMEM((tokens, 640), BF16),
            pltpu.VMEM((tokens, 5120), BF16),
            pltpu.VMEM((4, tokens, 1280), BF16),
            pltpu.VMEM((16, 2, 160, 640), BF16),
            pltpu.VMEM((16, 2, 160, 640), BF16),
            pltpu.VMEM((4, 144, 128), BF16),
            pltpu.VMEM((4, 2, 4 * columns, 896), BF16),
            pltpu.VMEM((320, 256), BF16),
            pltpu.VMEM((16, 16, PART, 128), BF16),
            pltpu.VMEM((8, PART + 8, 128), F32),
            pltpu.VMEM((7, PART + 8, 128), F32),
            pltpu.VMEM((tokens, 640), BF16),
            pltpu.VMEM((tokens, 640), F32),
            pltpu.VMEM((5, tokens, 128), BF16),
            pltpu.VMEM((5, tokens, 128), F32),
            pltpu.VMEM((5, tokens, 256), F32),
            pltpu.VMEM((tokens, 640), BF16),
            pltpu.VMEM((8, tokens, 640), BF16),
            pltpu.SemaphoreType.DMA((SENDS,)),
            pltpu.SemaphoreType.DMA((RECVS,)),
        ],
        compiler_params=pltpu.CompilerParams(
            collective_id=0, has_side_effects=True, vmem_limit_bytes=36 << 20),
    )(*[pltpu.with_memory_space_constraint(array, pltpu.HBM) for array in arrays])


def solution(mesh):
    return jax.shard_map(
        per_device,
        mesh=mesh,
        in_specs=(
            P("section", "ctx", None),
            P("ctx", None),
            P("ctx", None),
            P(None, ("section", "ctx")),
            P(("section", "ctx"), None),
            P("section", "ctx", None),
            P("section", None, "ctx"),
        ),
        out_specs=(P("section", "ctx", None), P("ctx", None)),
        check_vma=False,
    )
```

```python
import functools
import math

import jax
import jax.numpy as jnp
from jax import lax
from jax.experimental import pallas as pl
from jax.experimental.pallas import tpu as pltpu
from jax.sharding import PartitionSpec as P

MESH = pl.DeviceIdType.MESH
WINDOW = 128
F32 = jnp.float32
BF16 = jnp.bfloat16
NEG = -1e30

NT = (((1,), (1,)), ((), ()))
NN = (((1,), (0,)), ((), ()))

PART = 48
LOW = -1e20


def dot(a, b, dims=NN):
    return lax.dot_general(a, b, dims, preferred_element_type=F32)


class Place:
    def __init__(self):
        section = lax.axis_index("section")
        ctx = lax.axis_index("ctx")
        self.at = dict(zl=section // 4, y=section % 4, x=ctx // 8, zh=(ctx // 2) % 4, co=ctx % 2)
        self.ctx = ctx
        self.section = section

    SIZE = dict(zl=2, y=4, x=4, zh=4, co=2)

    def shifted(self, axis, step):
        size = self.SIZE[axis]
        return lax.rem(self.at[axis] + (step + size), size)

    def device(self, **steps):
        c = dict(self.at)
        for axis, step in steps.items():
            c[axis] = self.shifted(axis, step)
        return (c["zl"] * 4 + c["y"], (c["x"] * 4 + c["zh"]) * 2 + c["co"])

    def ctx_device(self, step):
        return (self.section, lax.rem(self.ctx + step + 32, 32))


class Copies:
    def __init__(self, send, recv):
        self.send, self.recv = send, recv
        self.sends, self.recvs = {}, {}

    def index(self, table, name):
        return table.setdefault(name, len(table))

    def remote(self, ref, device, send, recv, dst=None):
        pltpu.make_async_remote_copy(
            src_ref=ref, dst_ref=ref if dst is None else dst,
            send_sem=self.send.at[self.index(self.sends, send)],
            recv_sem=self.recv.at[self.index(self.recvs, recv)],
            device_id=device, device_id_type=MESH).start()

    def local(self, src, dst, send):
        pltpu.make_async_copy(src, dst, self.send.at[self.index(self.sends, send)]).start()

    def arrived(self, recv, like):
        pltpu.make_async_copy(like, like, self.recv.at[self.recvs[recv]]).wait()

    def left(self, send, like):
        pltpu.make_async_copy(like, like, self.send.at[self.sends[send]]).wait()


class Gather:
    def __init__(self, name, place, copies, buf, low, cut, high, first, second):
        self.name, self.place, self.copies, self.buf = name, place, copies, buf
        self.low, self.cut, self.high = low, cut, high
        self.first, self.second = first, second

    def put(self, key, i, j, low, high, axis, step):
        x, zh = (i, j) if self.first == "x" else (j, i)
        index = self.place.shifted("x", x) * 4 + self.place.shifted("zh", zh)
        ref = self.buf.at[index, self.place.at["co"], pl.ds(low, high - low)]
        self.copies.remote(ref, self.place.device(**{axis: step}), self.name, (self.name, key))

    def like(self, blocks):
        return self.buf.at[pl.ds(0, blocks), 0, pl.ds(self.low, self.high - self.low)]

    def got(self, key, blocks):
        self.copies.arrived((self.name, key), self.like(blocks))

    def start1(self):
        self.put("near", 0, 0, self.low, self.high, self.first, 1)
        self.put("near", 0, 0, self.low, self.high, self.first, -1)

    def forward1(self):
        self.got("near", 2)
        self.put("far", -1, 0, self.low, self.cut, self.first, 1)
        self.put("far", 1, 0, self.cut, self.high, self.first, -1)

    def start2(self, i):
        if i == 2:
            self.got("far", 1)
        self.put(("near", i), i, 0, self.low, self.high, self.second, 1)
        self.put(("near", i), i, 0, self.low, self.high, self.second, -1)

    def forward2(self, i):
        self.got(("near", i), 2)
        self.put(("far", i), i, -1, self.low, self.cut, self.second, 1)
        self.put(("far", i), i, 1, self.cut, self.high, self.second, -1)

    def finish2(self, i):
        self.got(("far", i), 1)

    def sent(self):
        self.copies.left(self.name, self.like(15))


class Swap:
    def __init__(self, name, place, copies, buf):
        self.name, self.place, self.copies, self.buf = name, place, copies, buf

    def put(self, x, ref):
        self.copies.remote(ref, self.place.device(co=1), (self.name, "swap"), (self.name, "swap", x))

    def rows(self, x, low, count):
        return self.buf.at[pl.ds(self.place.shifted("x", x) * 4, 4), self.place.at["co"], pl.ds(low, count)]

    def most(self, x):
        self.put(x, self.rows(x, 0, 128))

    def far(self, i):
        index = self.place.shifted("x", 2) * 4 + self.place.shifted("zh", i)
        self.put(2, self.buf.at[index, self.place.at["co"], pl.ds(0, 128)])

    def rest(self, x):
        self.put(x, self.rows(x, 128, 32))

    def done(self, x):
        self.copies.arrived((self.name, "swap", x), self.buf.at[pl.ds(0, 4), 0])


def eye_rows(rows, columns):
    return lax.broadcasted_iota(jnp.int32, (rows, columns), 0) == lax.broadcasted_iota(jnp.int32, (rows, columns), 1)


def spread(column, width):
    return jnp.broadcast_to(column, (column.shape[0], width))


def kernel(x_in, q_hbm, kv_in, so_in, kw_in, wq_in, wo_in, out, shared,
           q_in, xv, normed, wq, wo, sz, sw, near, kv, stage, gathered, window, qacc, queries, top, accum, cross, res,
           send, recv):
    place = Place()
    copies = Copies(send, recv)
    ctx = place.ctx
    at = place.at
    me = at["x"] * 4 + at["zh"]
    core = at["co"]
    rows = q_in.shape[0]
    heads = q_in.shape[1] // 128
    factor = 1.0 / math.sqrt(128)
    sibling = place.device(co=1)
    columns = so_in.shape[0]

    friends = [place.device(x=1), place.device(x=-1), place.device(x=2), place.device(zh=1), place.device(zh=-1),
               place.device(zh=2), sibling, place.ctx_device(1), place.ctx_device(-1)]
    for zl in (0, 1):
        for y in range(4):
            if zl or y:
                friends.append(place.device(zl=zl, y=y))
    barrier = pltpu.get_barrier_semaphore()
    for friend in friends:
        pl.semaphore_signal(barrier, inc=1, device_id=friend, device_id_type=MESH)

    copies.local(kv_in, near.at[pl.ds(128, rows)], "kv in")
    copies.local(wq_in.at[0], wq.at[me, core], "wq in")
    copies.local(q_hbm, q_in, "q in")
    copies.local(x_in.at[0], xv, "x in")
    copies.local(wo_in, wo.at[me, core], "wo in")

    sz[at["zh"], 112:144, :] = jnp.zeros((32, 128), BF16)
    for n in range(7):
        ref, lane = (so_in, n * 128) if n < 5 else (kw_in, (n - 5) * 128)
        sz[at["zh"], 16 * n:16 * n + 16, :] = ref[0:16, lane:lane + 128]
        sz[at["zh"], 112 + 4 * n:116 + 4 * n, :] = ref[16:20, lane:lane + 128]
    copies.left("kv in", near.at[pl.ds(128, rows)])
    copies.left("wq in", wq.at[me, core])
    pl.semaphore_wait(barrier, len(friends))

    qa = Gather("qa", place, copies, wq, 0, 64, 128, "zh", "x")
    qb = Gather("qb", place, copies, wq, 128, 144, 160, "x", "zh")
    oa = Gather("oa", place, copies, wo, 0, 64, 128, "zh", "x")
    ob = Gather("ob", place, copies, wo, 128, 144, 160, "x", "zh")
    half, y = at["zl"], at["y"]
    other = lax.rem(half + 1, 2)
    diagonal = eye_rows(PART, 128)

    def group(h, part, c):
        return (h * 4 + part) * 2 + c

    mine = group(half, y, core)

    q_swap = Swap("wq", place, copies, wq)
    o_swap = Swap("wo", place, copies, wo)

    def start():
        for k in (1, -1, 2):
            copies.remote(sz.at[at["zh"]], place.device(zh=k), "self z", "self z")
        copies.remote(near.at[pl.ds(192, 128)], place.ctx_device(1), "rim", "rim", near.at[pl.ds(0, 128)])

    def window_attention():
        copies.left("q in", q_in)
        copies.arrived("rim", near.at[pl.ds(0, 128)])
        qpos = lax.broadcasted_iota(jnp.int32, (rows, 320), 0)
        kpos = lax.broadcasted_iota(jnp.int32, (rows, 320), 1) - 128
        allowed = (kpos <= qpos) & (kpos > qpos - WINDOW) & (kpos >= -rows * ctx)
        for h in range(heads):
            scores = dot(q_in[:, h * 128:(h + 1) * 128], near[:, 0:128], NT) * factor
            scores = jnp.where(allowed, scores, NEG)
            expo = jnp.exp(scores - jnp.max(scores, axis=1, keepdims=True))
            numer = dot(expo.astype(BF16), near[:, 128:256])
            window[:, h * 128:(h + 1) * 128] = (numer / jnp.sum(expo, axis=1, keepdims=True)).astype(BF16)

    def self_x():
        copies.arrived("self z", sz.at[pl.ds(0, 3)])
        for k in range(4):
            for n in range(7):
                lanes = slice(n * 128, n * 128 + 128)
                sw[at["x"], core, k * 20:k * 20 + 16, lanes] = sz[k, 16 * n:16 * n + 16, :]
                sw[at["x"], core, k * 20 + 16:k * 20 + 20, lanes] = sz[k, 112 + 4 * n:116 + 4 * n, :]
        own = sw.at[at["x"], core]
        for k in (1, -1, 2):
            copies.remote(own, place.device(x=k), "self x", "self x")
        copies.remote(own, sibling, "self swap", "self swap")

    def self_swap():
        copies.arrived("self x", sw.at[pl.ds(0, 3), 0])
        for k in (1, -1, 2):
            copies.remote(sw.at[place.shifted("x", k), core], sibling, "self swap", "self swap")

    def mix():
        copies.arrived("self swap", sw.at[:, 0])
        weights = sw[...].reshape(32 * columns, 896)
        mixed = dot(window[...], weights[:, 0:640], NT).astype(BF16)
        wide = mixed.astype(F32)
        squares = jnp.sum(wide * wide, axis=1, keepdims=True)
        raw = dot(mixed, weights[:, 640:896])
        for s in range(8):
            part, side = s % 4, s // 4
            stage[s, 0:PART] = raw[part * PART:(part + 1) * PART, side * 128:(side + 1) * 128]
            line = jnp.sum(jnp.where(diagonal, squares[part * PART:(part + 1) * PART], 0.0), axis=0, keepdims=True)
            stage[s, PART:PART + 8] = jnp.broadcast_to(line, (8, 128))
        for zl in (0, 1):
            for k in range(4):
                if zl or k:
                    to = place.device(zl=zl, y=k)
                    copies.remote(stage.at[to[0]], to, "reduce", "reduce", gathered.at[zl * 4 + k - 1])

    def reduce():
        copies.arrived("reduce", gathered)
        summed = stage[place.section]
        for slot in range(7):
            summed = summed + gathered[slot]
        column = jnp.sum(jnp.where(diagonal, summed[PART:PART + 1], 0.0), axis=1, keepdims=True)
        kv[mine, me] = (summed[0:PART] * lax.rsqrt(column / 5120.0 + 1e-6)).astype(BF16)
        for k in (1, -1, 2):
            copies.remote(kv.at[mine, me], place.device(zh=k), "kv piece", "kv z")

    def kv_x():
        copies.arrived("kv z", kv.at[0, pl.ds(0, 3)])
        for k in (1, -1, 2):
            copies.remote(kv.at[mine, pl.ds(at["x"] * 4, 4)], place.device(x=k), "kv piece", "kv x")

    def round_start(h):
        for k in (1, -1):
            copies.remote(kv.at[group(h, y, core)], place.device(y=k), "kv group", ("kv near", h is half))

    def hand(h, part, batch):
        copies.remote(kv.at[group(h, part, core)], sibling, "kv swap", ("kv swap", batch))

    def kv_round():
        copies.arrived("kv x", kv.at[0, pl.ds(0, 12)])
        copies.remote(kv.at[mine], place.device(zl=1), "kv group", "kv across")
        round_start(half)
        hand(half, y, 0)

    def kv_across():
        copies.arrived("kv across", kv.at[0])
        round_start(other)
        hand(other, y, 0)

    def round_forward(h):
        copies.arrived(("kv near", h is half), kv.at[pl.ds(0, 2)])
        copies.remote(kv.at[group(h, place.shifted("y", -1), core), pl.ds(0, 8)], place.device(y=1),
                      "kv group", ("kv far", h is half))
        copies.remote(kv.at[group(h, place.shifted("y", 1), core), pl.ds(8, 8)], place.device(y=-1),
                      "kv group", ("kv far", h is half))
        for k in (1, -1):
            hand(h, place.shifted("y", k), 1)

    def round_end(h):
        copies.arrived(("kv far", h is half), kv.at[0])
        hand(h, place.shifted("y", 2), 2)

    def normalise():
        copies.left("x in", xv)

        def norm_rows(i, carry):
            block = pl.ds(pl.multiple_of(i * 16, 16), 16)
            hidden = xv[block, :].astype(F32)
            scale = lax.rsqrt(jnp.sum(hidden * hidden, axis=1, keepdims=True) / hidden.shape[1] + 1e-6)
            hidden = (hidden * scale).astype(BF16)
            for g in range(4):
                normed[g, block, :] = hidden[:, g * 1280:(g + 1) * 1280]
            return carry

        lax.fori_loop(0, rows // 16, norm_rows, 0, unroll=3)

    seen = []

    def query_product(x):
        q_swap.done(x)
        where = place.shifted("x", x)
        product = dot(normed[where], wq[pl.ds(where * 4, 4)].reshape(1280, 640))
        if seen:
            qacc[...] += product
        else:
            qacc[...] = product
        seen.append(x)

    def finish_queries():
        scaled = (qacc[...] * factor).astype(BF16)
        for h in range(heads):
            queries[h] = scaled[:, h * 128:(h + 1) * 128]
        top[...] = jnp.full_like(top, LOW)
        accum[...] = jnp.zeros_like(accum)

    def handed(batch):
        copies.arrived(("kv swap", batch), kv.at[pl.ds(0, 4 if batch == 1 else 2)])

    def attend(k, c):
        part = place.shifted("y", k)
        lane = lax.broadcasted_iota(jnp.int32, (1, 16 * PART), 1)
        chip = jnp.zeros_like(lane)
        for n in range(1, 16):
            chip = chip + (lane >= n * PART).astype(jnp.int32)
        position = chip * (2 * rows - PART) + lane + (c * rows + part * PART)
        row = lax.broadcasted_iota(jnp.int32, (rows, 1), 0) + ctx * rows
        bias = jnp.where(position <= row, 0.0, NEG)
        keys = kv[group(0, part, c)].reshape(16 * PART, 128)
        values = kv[group(1, part, c)].reshape(16 * PART, 128)
        both = jnp.concatenate([values, jnp.ones((16 * PART, 128), BF16)], axis=1)
        for h in range(heads):
            scores = dot(queries[h], keys, NT) + bias
            old = top[h]
            new = jnp.maximum(old, spread(jnp.max(scores, axis=1, keepdims=True), 128))
            expo = jnp.exp(scores - jnp.tile(new, (1, 6)))
            fade = jnp.exp(old - new)
            accum[h] = accum[h] * jnp.tile(fade, (1, 2)) + dot(expo.astype(BF16), both)
            top[h] = new

    def finish_cross():
        for h in range(heads):
            cross[:, h * 128:(h + 1) * 128] = (accum[h, :, 0:128] / accum[h, :, 128:256]).astype(BF16)
        for k in range(4):
            shared[k * PART:(k + 1) * PART, 0:128] = kv[group(0, k, core), me]
            shared[k * PART:(k + 1) * PART, 128:256] = kv[group(1, k, core), me]

    def update(x):
        o_swap.done(x)
        where = place.shifted("x", x)
        for pair in range(2):
            w = wo[pl.ds(where * 4 + 2 * pair, 2)].reshape(640, 640)
            slot = (x % 4) * 2 + pair
            res[slot] = dot(cross[...], w, NT).astype(BF16)
            block = pl.ds(pl.multiple_of((where * 2 + pair) * 640, 640), 640)
            copies.local(res.at[slot], out.at[0, :, block], "out")

    start()
    copies.left("wo in", wo.at[me, core])
    oa.start2(0)
    qa.start2(0)
    qb.start1()
    ob.start1()
    qa.start1()
    normalise()
    self_x()
    oa.forward2(0)
    window_attention()
    qa.forward2(0)
    qb.forward1()
    qb.start2(-1)
    ob.forward1()
    qb.start2(0)
    qb.start2(1)
    qb.forward2(-1)
    qa.forward1()
    self_swap()
    qa.start2(-1)
    qa.start2(1)
    mix()
    qb.finish2(-1)
    q_swap.rest(-1)
    oa.finish2(0)
    o_swap.far(0)
    qa.finish2(0)
    q_swap.far(0)
    qb.forward2(1)
    qb.forward2(0)
    qb.start2(2)
    qa.start2(2)
    q_swap.most(0)
    reduce()
    qb.finish2(1)
    q_swap.rest(1)
    qb.finish2(0)
    q_swap.rest(0)
    oa.start1()
    query_product(0)
    qa.forward2(-1)
    kv_x()
    qa.forward2(1)
    qa.forward2(2)
    q_swap.most(-1)
    q_swap.most(1)
    qb.forward2(2)
    qa.finish2(-1)
    q_swap.far(-1)
    query_product(-1)
    ob.start2(0)
    query_product(1)
    kv_round()
    oa.forward1()
    oa.start2(-1)
    oa.start2(1)
    qb.finish2(2)
    q_swap.rest(2)
    qa.finish2(1)
    q_swap.far(1)
    qa.finish2(2)
    q_swap.far(2)
    ob.start2(-1)
    query_product(2)
    finish_queries()
    kv_across()
    attend(0, core)
    handed(0)
    attend(0, 1 - core)
    oa.forward2(-1)
    round_forward(half)
    ob.forward2(0)
    oa.start2(2)
    o_swap.most(0)
    ob.start2(1)
    ob.start2(2)
    oa.forward2(1)
    ob.forward2(-1)
    round_forward(other)
    attend(1, core)
    ob.finish2(0)
    o_swap.rest(0)
    oa.finish2(-1)
    o_swap.far(-1)
    handed(1)
    attend(-1, 1 - core)
    ob.forward2(1)
    round_end(half)
    attend(1, 1 - core)
    round_end(other)
    ob.forward2(2)
    oa.forward2(2)
    ob.finish2(-1)
    o_swap.rest(-1)
    attend(2, core)
    handed(2)
    attend(2, 1 - core)
    ob.finish2(1)
    o_swap.rest(1)
    oa.finish2(1)
    o_swap.far(1)
    o_swap.most(1)
    o_swap.most(-1)
    attend(-1, core)
    ob.finish2(2)
    o_swap.rest(2)
    finish_cross()
    update(0)
    update(1)
    oa.finish2(2)
    o_swap.far(2)
    update(-1)
    update(2)

    for gather in (qa, qb, oa, ob):
        gather.sent()
    copies.left(("wq", "swap"), wq.at[:, 0])
    copies.left(("wo", "swap"), wo.at[:, 0])
    copies.left("self z", sz.at[pl.ds(0, 3)])
    copies.left("self x", sw.at[pl.ds(0, 3), 0])
    copies.left("self swap", sw.at[:, 0])
    copies.left("rim", near.at[pl.ds(0, 128)])
    copies.left("reduce", gathered)
    copies.left("kv piece", kv.at[0, pl.ds(0, 15)])
    copies.left("kv group", kv.at[pl.ds(0, 7)])
    copies.left("kv swap", kv.at[pl.ds(0, 8)])
    copies.left("out", res)
    assert (len(copies.sends), len(copies.recvs)) == (SENDS, RECVS), (len(copies.sends), len(copies.recvs))


SENDS = 20
RECVS = 63


def per_device(layer_input, self_q, self_kv, self_out_weight, kv_weight, q_weight, out_weight):
    vmem = pl.BlockSpec(memory_space=pltpu.VMEM)
    hbm = pl.BlockSpec(memory_space=pltpu.HBM)
    free = pl.BlockSpec(memory_space=pl.ANY)
    tokens = self_q.shape[0]
    columns = kv_weight.shape[0]
    arrays = (layer_input, self_q, self_kv, self_out_weight.T, kv_weight, q_weight, out_weight[0].T)
    return pl.pallas_call(
        kernel,
        name="layer_group",
        out_shape=(jax.ShapeDtypeStruct((1, tokens, 5120), BF16), jax.ShapeDtypeStruct((tokens, 256), BF16)),
        in_specs=[hbm, hbm, hbm, vmem, vmem, hbm, hbm],
        out_specs=(free, vmem),
        scratch_shapes=[
            pltpu.VMEM((tokens, 640), BF16),
            pltpu.VMEM((tokens, 5120), BF16),
            pltpu.VMEM((4, tokens, 1280), BF16),
            pltpu.VMEM((16, 2, 160, 640), BF16),
            pltpu.VMEM((16, 2, 160, 640), BF16),
            pltpu.VMEM((4, 144, 128), BF16),
            pltpu.VMEM((4, 2, 4 * columns, 896), BF16),
            pltpu.VMEM((320, 256), BF16),
            pltpu.VMEM((16, 16, PART, 128), BF16),
            pltpu.VMEM((8, PART + 8, 128), F32),
            pltpu.VMEM((7, PART + 8, 128), F32),
            pltpu.VMEM((tokens, 640), BF16),
            pltpu.VMEM((tokens, 640), F32),
            pltpu.VMEM((5, tokens, 128), BF16),
            pltpu.VMEM((5, tokens, 128), F32),
            pltpu.VMEM((5, tokens, 256), F32),
            pltpu.VMEM((tokens, 640), BF16),
            pltpu.VMEM((8, tokens, 640), BF16),
            pltpu.SemaphoreType.DMA((SENDS,)),
            pltpu.SemaphoreType.DMA((RECVS,)),
        ],
        compiler_params=pltpu.CompilerParams(
            collective_id=0, has_side_effects=True, vmem_limit_bytes=36 << 20),
    )(*[pltpu.with_memory_space_constraint(array, pltpu.HBM) for array in arrays])


def solution(mesh):
    return jax.shard_map(
        per_device,
        mesh=mesh,
        in_specs=(
            P("section", "ctx", None),
            P("ctx", None),
            P("ctx", None),
            P(None, ("section", "ctx")),
            P(("section", "ctx"), None),
            P("section", "ctx", None),
            P("section", None, "ctx"),
        ),
        out_specs=(P("section", "ctx", None), P("ctx", None)),
        check_vma=False,
    )
```
